512 devices in a mesh: segment: 16 (over y, z_lo), tensor: 32 (over z_hi, x, core).
Axes of the slice: x: 4, y: 8, z: 8 (z_hi: 4, z_lo: 2; z = z_hi * 2 + z_lo), core: 2. Of those that a mesh axis runs over, the one named last changes fastest.
Arguments:
- entering: bfloat16 [16, 128, 6144], P('segment', None, 'tensor'), may hold values from -6 to 6
- fresh_rows: bfloat16 [1, 128, 6144], P(None, None, 'tensor'), may hold values from -6 to 6
- norm_gain: float32 [16, 6144], P('segment'), may hold values from 0.1 to 1.9
- segment_weight: bfloat16 [16, 6144, 6144], P('segment', 'tensor'), may hold values from -0.078125 to 0.078125
- projection: bfloat16 [6144, 9216], P('segment', 'tensor'), may hold values from -0.078125 to 0.078125
- teacher_rows: bfloat16 [16, 2, 128, 9216], P('segment', None, None, 'tensor'), may hold values from -6 to 6
Outputs:
- leaving: bfloat16 [16, 128, 6144], P('segment', None, 'tensor')
- projection_grad: float32 [6144, 9216], P('segment', 'tensor')
The draws below stay inside these ranges and needn't reach their ends.
All inputs are finite; a program needn't handle non-finite values.
Results may differ from the reference program's by a relative error of at most 0.018.
Values may be sent and summed in bfloat16 or wider, within the bound.
No kernel may reach another device: no remote copies, remote signals or barrier semaphores. Data moves between devices by JAX's collectives and lax.ppermute only.
A program may use at most 64 MiB of HBM per device.

```python
import jax
import jax.numpy as jnp
from jax import lax

DS = 6144
DTW = 9216
ROWS = 128
TICKS = 2
SEGMENTS = 16
N_SEGMENT = 16


def level_of(rng, dims, pieces, low, largest):
    loudness, own = 1.0, jax.random.fold_in(rng, 6)
    for position, parts in pieces:
        heights = jnp.exp(jax.random.uniform(jax.random.fold_in(own, position), (parts,), jnp.float32, low / len(pieces), largest / len(pieces)))
        loudness = loudness * jnp.repeat(heights, dims[position] // parts).reshape([-1 if axis == position else 1 for axis in range(len(dims))])
    return loudness


def gaussian(stream_key, shape, scale, bound, shards=(), kind=jnp.bfloat16):
    entries = jax.random.normal(stream_key, shape, jnp.float32) * scale
    if len(shards) > 0:
        entries = level_of(stream_key, shape, shards, -0.22, 0.18) * entries
    return jnp.clip(entries, min=-bound, max=bound).astype(kind)


def setup_inputs(seed: int = 0) -> dict:
    key_of = jax.random.split(jax.random.key(seed), 7)
    return {
        "entering": gaussian(key_of[0], (SEGMENTS, ROWS, DS), 1.0, 6.0, ((0, 16), (2, 32))),
        "fresh_rows": gaussian(key_of[1], (TICKS - 1, ROWS, DS), 1.0, 6.0, ((2, 32),)),
        "norm_gain": jnp.clip(1.0 + 0.18 * jax.random.normal(key_of[2], (SEGMENTS, DS), jnp.float32), 0.1, 1.9),
        "segment_weight": gaussian(key_of[3], (SEGMENTS, DS, DS), DS ** -0.5, 0.078125, ((0, 16), (1, 32))),
        "projection": gaussian(key_of[4], (DS, DTW), DS ** -0.5, 0.078125, ((0, 16), (1, 32))),
        "teacher_rows": gaussian(key_of[5], (SEGMENTS, TICKS, ROWS, DTW), 1.0, 6.0, ((0, 16), (3, 32))),
    }


EPSILON = 1e-05

def segment_forward(inputs, scales, weights):
    full_float = inputs.astype(jnp.float32)
    mean_square = lax.optimization_barrier(jnp.mean(full_float * full_float, axis=-1, keepdims=True))
    normed = (full_float * lax.rsqrt(mean_square + EPSILON) * scales[None, :]).astype(jnp.bfloat16)
    hidden_sum = lax.dot_general(normed, weights, (((1,), (1,)), ((), ())), preferred_element_type=jnp.float32)
    return (full_float + jax.nn.silu(hidden_sum)).astype(jnp.bfloat16)

def reference(entering, fresh_rows, norm_gain, segment_weight, projection, teacher_rows):
    current_rows = entering
    outputs = entering
    kept_rows = []
    kept_diffs = []
    for tick_index in range(TICKS):
        if tick_index > 0:
            current_rows = jnp.concatenate([fresh_rows[tick_index - 1][None], outputs[:-1]], axis=0)
        outputs = lax.map(lambda operands: segment_forward(operands[0], operands[1], operands[2]), (current_rows, norm_gain, segment_weight))
        flat_rows = outputs.reshape(N_SEGMENT * ROWS, DS)
        predicted = jnp.dot(flat_rows, projection, preferred_element_type=jnp.float32)
        targets = teacher_rows[:, tick_index].reshape(N_SEGMENT * ROWS, DTW).astype(jnp.float32)
        difference = (predicted - targets).astype(jnp.bfloat16).reshape(N_SEGMENT, ROWS, DTW)
        kept_rows.append(outputs)
        kept_diffs.append(difference)
    all_rows = jnp.stack(kept_rows, axis=1).reshape(N_SEGMENT, TICKS * ROWS, DS)
    all_diffs = jnp.stack(kept_diffs, axis=1).reshape(N_SEGMENT, TICKS * ROWS, DTW)
    scale_factor = 1.0 / (TICKS * ROWS)

    def accumulate(running_sum, operands):
        rows_block, diff_block = operands
        segment_term = lax.dot_general(rows_block, diff_block, (((0,), (0,)), ((), ())), preferred_element_type=jnp.float32)
        rounded = lax.optimization_barrier((segment_term * scale_factor).astype(jnp.bfloat16))
        return (running_sum + rounded.astype(jnp.float32), None)
    running_sum, unused = lax.scan(accumulate, jnp.zeros((DS, DTW), jnp.float32), (all_rows, all_diffs))
    return (outputs, running_sum)
```

```python
import functools

import jax
import jax.numpy as jnp
from jax import lax
from jax.experimental import pallas as pl
from jax.experimental.pallas import tpu as pltpu
from jax.sharding import PartitionSpec as P

EPSILON = 1e-05
TICKS = 2
NZ, NX, NC, NY = 4, 4, 2, 8
ROWS = 128
PIECE = 192
WIDTH = 6144
COLS = 288
BLOCK = 384
ORDER = (0, 8, 4, 12, 1, 9, 5, 13, 2, 10, 6, 14, 3, 11, 7, 15)
VMEM_LIMIT = 48 * 1024 * 1024
SMEM_SPEC = pl.BlockSpec(memory_space=pltpu.SMEM)
VMEM_SPEC = pl.BlockSpec(memory_space=pltpu.VMEM)


def t_index(z, x, c):
    return (z % NZ) * 8 + (x % NX) * 2 + c % NC


Z_GROUPS = [[t_index(z, x, c) for z in range(NZ)] for x in range(NX) for c in range(NC)]
X_GROUPS = [[t_index(z, x, c) for x in range(NX)] for z in range(NZ) for c in range(NC)]
Y_GROUPS = [[(2 * i + par) * 2 + zl for i in range(4)] for par in range(2) for zl in range(2)]


def all_t():
    return [(z, x, c) for z in range(NZ) for x in range(NX) for c in range(NC)]


def over_tensor(value, move):
    return lax.ppermute(value, "tensor", [(t_index(*p), t_index(*move(*p))) for p in all_t()])


def over_segment(value, mask):
    return lax.ppermute(value, "segment", [(i, i ^ mask) for i in range(16)])


def z_gather(value):
    return lax.all_gather(value, "tensor", axis=0, tiled=True, axis_index_groups=Z_GROUPS)


def x_gather(value):
    return lax.all_gather(value, "tensor", axis=0, tiled=True, axis_index_groups=X_GROUPS)


def core_swap(value):
    return over_tensor(value, lambda z, x, c: (z, x, c + 1))


def x_relative(value):
    got = [over_tensor(value, lambda z, x, c, k=k: (z, x - k, c)) for k in (1, 2, 3)]
    return jnp.concatenate([value] + got, axis=0)


def transposition():
    pairs = []
    for yy in range(NY):
        for zl in range(2):
            for z, x, c in all_t():
                y = z * 2 + (x >> 1)
                there = t_index(yy >> 1, (yy & 1) * 2 + (x & 1), c)
                pairs.append(((yy * 2 + zl) * 32 + t_index(z, x, c), (y * 2 + zl) * 32 + there))
    return pairs


def scaled_weights(weights, gain):
    return (weights.astype(jnp.float32) * gain).astype(jnp.bfloat16)


def tick_kernel(where_ref, own_ref, other_ref, weight_ref, mine_ref, out_ref, full):
    core = where_ref[0]
    square = jnp.zeros((8, ROWS), jnp.float32)
    for x in range(NX):
        for z in range(NZ):
            base = t_index(z, x, 0) * PIECE
            source = pl.ds((x * NZ + z) * PIECE, PIECE)
            for ref, c in ((own_ref, core), (other_ref, 1 - core)):
                piece = ref[source, :]
                full[pl.ds(pl.multiple_of(base + c * PIECE, PIECE), PIECE), :] = piece
                wide = piece.astype(jnp.float32)
                square += jnp.sum((wide * wide).reshape(PIECE // 8, 8, ROWS), axis=0)
    mean_square = jnp.sum(square, axis=0, keepdims=True) * (1.0 / WIDTH)
    scale = lax.rsqrt(mean_square + EPSILON)
    hidden = jnp.dot(weight_ref[...], full[...], preferred_element_type=jnp.float32) * scale
    silu = hidden / (1.0 + jnp.exp(-hidden))
    out_ref[...] = (mine_ref[...].astype(jnp.float32) + silu).astype(jnp.bfloat16)


def tick(where, own, other, weights, mine):
    return pl.pallas_call(
        tick_kernel,
        out_shape=jax.ShapeDtypeStruct((PIECE, ROWS), jnp.bfloat16),
        in_specs=[SMEM_SPEC] + [VMEM_SPEC] * 4,
        out_specs=VMEM_SPEC,
        scratch_shapes=[pltpu.VMEM((WIDTH, ROWS), jnp.bfloat16)],
        compiler_params=pltpu.CompilerParams(vmem_limit_bytes=VMEM_LIMIT),
        name="tick",
    )(where, own, other, weights, mine)


def predict_kernel(where_ref, own_ref, other_ref, block_ref, teacher_ref, out_ref, full):
    core, segment, x_mine = where_ref[0], where_ref[1], where_ref[2]
    for k in range(NX):
        x = (x_mine + k) % NX
        for z in range(NZ):
            for tau in range(TICKS):
                source = pl.ds(((k * NZ + z) * TICKS + tau) * PIECE, PIECE)
                for ref, c in ((own_ref, core), (other_ref, 1 - core)):
                    at = pl.multiple_of((z * 8 + x * 2 + c) * PIECE, PIECE)
                    full[pl.ds(at, PIECE), tau * ROWS : (tau + 1) * ROWS] = ref[source, :]
    total = jnp.zeros((COLS, TICKS * ROWS), jnp.float32)
    for j, mask in enumerate(ORDER):
        at = pl.multiple_of((segment ^ mask) * BLOCK, BLOCK)
        total += jnp.dot(
            block_ref[j * COLS : (j + 1) * COLS, :],
            full[pl.ds(at, BLOCK), :],
            preferred_element_type=jnp.float32,
        )
    for tau in range(TICKS):
        taught = teacher_ref[tau].astype(jnp.float32)
        difference = total[:, tau * ROWS : (tau + 1) * ROWS] - taught
        out_ref[tau * COLS : (tau + 1) * COLS, :] = difference.astype(jnp.bfloat16)


def predict(where, own, other, blocks, teacher):
    return pl.pallas_call(
        predict_kernel,
        out_shape=jax.ShapeDtypeStruct((TICKS * COLS, ROWS), jnp.bfloat16),
        in_specs=[SMEM_SPEC] + [VMEM_SPEC] * 4,
        out_specs=VMEM_SPEC,
        scratch_shapes=[pltpu.VMEM((WIDTH, TICKS * ROWS), jnp.bfloat16)],
        compiler_params=pltpu.CompilerParams(vmem_limit_bytes=VMEM_LIMIT),
        name="predict",
    )(where, own, other, blocks, teacher)


def gradient_kernel(where_ref, near_ref, far_ref, own_ref, other_ref, keep_ref, send_ref, rows, diffs):
    core, segment, x_mine = where_ref[0], where_ref[1], where_ref[2]
    parity, half = (segment >> 1) & 1, segment & 1
    for i in range(4):
        for ref, p in ((near_ref, parity), (far_ref, 1 - parity)):
            for tau in range(TICKS):
                source = pl.ds((i * TICKS + tau) * COLS, COLS)
                diffs[2 * i + p, :, tau * ROWS : (tau + 1) * ROWS] = ref[source, :]
    for k in range(NX):
        x = (x_mine + k) % NX
        for z in range(NZ):
            y = z * 2 + (x >> 1)
            for ref, c in ((own_ref, core), (other_ref, 1 - core)):
                at = pl.multiple_of(((x & 1) * 2 + c) * PIECE, PIECE)
                for tau in range(TICKS):
                    source = pl.ds(((k * NZ + z) * TICKS + tau) * PIECE, PIECE)
                    rows[y, pl.ds(at, PIECE), tau * ROWS : (tau + 1) * ROWS] = ref[source, :]
    for part, ref in ((half, keep_ref), (1 - half, send_ref)):
        total = jnp.zeros((COLS, BLOCK), jnp.float32)
        for y in range(NY):
            total += lax.dot_general(
                diffs[y],
                rows[y, pl.ds(pl.multiple_of(part * BLOCK, BLOCK), BLOCK), :],
                (((1,), (1,)), ((), ())),
                preferred_element_type=jnp.float32,
            )
        ref[...] = (total * (1.0 / (TICKS * ROWS))).astype(ref.dtype)


def gradient(where, near, far, own, other):
    return pl.pallas_call(
        gradient_kernel,
        out_shape=(
            jax.ShapeDtypeStruct((COLS, BLOCK), jnp.float32),
            jax.ShapeDtypeStruct((COLS, BLOCK), jnp.bfloat16),
        ),
        in_specs=[SMEM_SPEC] + [VMEM_SPEC] * 4,
        out_specs=(VMEM_SPEC, VMEM_SPEC),
        scratch_shapes=[
            pltpu.VMEM((NY, 2 * BLOCK, TICKS * ROWS), jnp.bfloat16),
            pltpu.VMEM((NY, COLS, TICKS * ROWS), jnp.bfloat16),
        ],
        compiler_params=pltpu.CompilerParams(vmem_limit_bytes=VMEM_LIMIT),
        name="gradient",
    )(where, near, far, own, other)


def on_device(entering, fresh_rows, norm_gain, segment_weight, projection, teacher_rows):
    t, segment = lax.axis_index("tensor"), lax.axis_index("segment")
    where = jnp.stack([t & 1, segment, (t >> 1) & 3]).astype(jnp.int32)
    weights = scaled_weights(segment_weight[0], norm_gain)
    teacher = teacher_rows[0].swapaxes(1, 2)

    blocks = projection.T
    for mask in (8, 4, 1, 2):
        blocks = jnp.concatenate([blocks, over_segment(blocks, mask)], axis=0)

    entering_t, fresh_t = entering[0].T, fresh_rows[0].T
    first = z_gather(jnp.concatenate([entering_t, fresh_t], axis=0)).reshape(NZ, 2, PIECE, ROWS)
    own = x_gather(first[:, 0].reshape(NZ * PIECE, ROWS))
    out0 = tick(where, own, core_swap(own), weights, entering_t)

    shifted = lax.ppermute(out0, "segment", [(i, i + 1) for i in range(15)])
    mine = jnp.where(segment == 0, fresh_t, shifted)
    column = z_gather(mine)
    own = x_gather(column)
    out1 = tick(where, own, core_swap(own), weights, mine)

    both = jnp.concatenate([out0, out1], axis=0)
    turned = lax.ppermute(both, ("segment", "tensor"), transposition())
    own = x_relative(z_gather(both))
    difference = predict(where, own, core_swap(own), blocks, teacher)

    own_rows = x_relative(z_gather(turned))
    other_rows = core_swap(own_rows)
    near = lax.all_gather(difference, "segment", axis=0, tiled=True, axis_index_groups=Y_GROUPS)
    far = over_segment(near, 2)
    keep, send = gradient(where, near, far, own_rows, other_rows)
    got = over_segment(send, 1)
    total = keep + got.astype(jnp.float32)
    return (out1.T[None], total.T)


def solution(mesh):
    return jax.shard_map(
        on_device,
        mesh=mesh,
        in_specs=(
            P("segment", None, "tensor"),
            P(None, None, "tensor"),
            P("segment", None),
            P("segment", "tensor", None),
            P("segment", "tensor"),
            P("segment", None, None, "tensor"),
        ),
        out_specs=(P("segment", None, "tensor"), P("segment", "tensor")),
        check_vma=False,
    )
```

```python
import jax
import jax.numpy as jnp
from jax import lax
from jax.experimental import pallas as pl
from jax.experimental.pallas import tpu as pltpu
from jax.sharding import PartitionSpec as P

EPSILON = 1e-05
TICKS = 2
NZ, NX, NC, NY = 4, 4, 2, 8
ROWS = 128
PIECE = 192
WIDTH = 6144
COLS = 288
BLOCK = 384
MASKS = (0, 1, 3, 2)
VMEM_LIMIT = 48 * 1024 * 1024
SMEM_SPEC = pl.BlockSpec(memory_space=pltpu.SMEM)
VMEM_SPEC = pl.BlockSpec(memory_space=pltpu.VMEM)


def t_index(z, x, c):
    return (z % NZ) * 8 + (x % NX) * 2 + c % NC


def all_t():
    return [(z, x, c) for z in range(NZ) for x in range(NX) for c in range(NC)]


def over_tensor(value, move):
    return lax.ppermute(value, "tensor", [(t_index(*p), t_index(*move(*p))) for p in all_t()])


def over_y(value, move):
    return lax.ppermute(
        value, "segment", [(y * 2 + zl, (move(y) % NY) * 2 + zl) for y in range(NY) for zl in range(2)]
    )


def z_swap(value, mask):
    return over_tensor(value, lambda z, x, c: (z ^ mask, x, c))


def x_swap(value, mask):
    return over_tensor(value, lambda z, x, c: (z, x ^ mask, c))


def core_swap(value):
    return over_tensor(value, lambda z, x, c: (z, x, c ^ 1))


def zl_swap(value):
    return lax.ppermute(value, "segment", [(i, i ^ 1) for i in range(16)])


def to_next_segment(value, mask):
    pairs = []
    for s in range(16):
        for z, x, c in all_t():
            pairs.append((s * 32 + t_index(z, x, c), ((s + 1) % 16) * 32 + t_index(z ^ mask, x, c)))
    return lax.ppermute(value, ("segment", "tensor"), pairs)


def transposition(value):
    pairs = []
    for yy in range(NY):
        for zl in range(2):
            for z, x, c in all_t():
                y = z * 2 + (x >> 1)
                there = t_index(yy >> 1, (yy & 1) * 2 + (x & 1), c)
                pairs.append(((yy * 2 + zl) * 32 + t_index(z, x, c), (y * 2 + zl) * 32 + there))
    return lax.ppermute(value, ("segment", "tensor"), pairs)


def stack(*values):
    return jnp.concatenate(values, axis=0)


def z_direct(value):
    return stack(value, *[z_swap(value, mask) for mask in MASKS[1:]])


def z_pairs(value):
    two = stack(value, z_swap(value, 1))
    return stack(two, z_swap(two, 3))


def x_and_core(value):
    near = stack(value, x_swap(value, 1))
    far = x_swap(near, 3)
    return near, far, core_swap(near), core_swap(far)


def other_neighbour(y):
    return y - 1 if y % 2 == 0 else y + 1


def y_gather(value):
    pair = stack(value, over_y(value, lambda y: y ^ 1))
    second = over_y(pair, other_neighbour)
    third = over_y(second, lambda y: y ^ 1)
    fourth = over_y(second, lambda y: y + 2 if y % 2 == 0 else y - 2)
    return pair, second, third, fourth


def y_labels(y):
    def other(v):
        return lax.rem(v + jnp.where(lax.rem(v, 2) == 0, NY - 1, 1), NY)

    away = lax.rem(y + jnp.where(lax.rem(y, 2) == 0, NY - 2, 2), NY)
    return y, other(y), other(y ^ 1), other(away)


def scaled_weights(weights, gain):
    return (weights.astype(jnp.float32) * gain).astype(jnp.bfloat16)


def pieces(where_ref, parts):
    core, z_mine, x_mine = where_ref[0], where_ref[2], where_ref[3]
    for ref, far, c in zip(parts, (0, 1, 0, 1), (core, core, core ^ 1, core ^ 1), strict=True):
        for i in range(2):
            for j in range(NZ):
                yield ref, i * NZ + j, z_mine ^ MASKS[j], x_mine ^ MASKS[2 * far + i], c


def feature_start(z, x, c):
    return pl.multiple_of((z * 8 + x * 2 + c) * PIECE, PIECE)


def tick_kernel(where_ref, *refs):
    parts, (weight_ref, mine_ref, out_ref, full, square) = refs[:-5], refs[-5:]

    def fill(four):
        square[...] = jnp.zeros((8, ROWS), jnp.float32)
        for ref, k, z, x, c in pieces(where_ref, four):
            piece = ref[k * PIECE : (k + 1) * PIECE, :]
            full[pl.ds(feature_start(z, x, c), PIECE), :] = piece
            wide = piece.astype(jnp.float32)
            square[...] += jnp.sum((wide * wide).reshape(PIECE // 8, 8, ROWS), axis=0)

    if len(parts) == 4:
        fill(parts)
    else:
        first = where_ref[1] == 0

        @pl.when(first)
        def _():
            fill(parts[4:])

        @pl.when(jnp.logical_not(first))
        def _():
            fill(parts[:4])

    mean_square = jnp.sum(square[...], axis=0, keepdims=True) * (1.0 / WIDTH)
    scale = lax.rsqrt(mean_square + EPSILON)
    hidden = jnp.dot(weight_ref[...], full[...], preferred_element_type=jnp.float32) * scale
    silu = hidden / (1.0 + jnp.exp(-hidden))
    out_ref[...] = (mine_ref[...].astype(jnp.float32) + silu).astype(jnp.bfloat16)


def tick(where, parts, weights, mine):
    return pl.pallas_call(
        tick_kernel,
        out_shape=jax.ShapeDtypeStruct((PIECE, ROWS), jnp.bfloat16),
        in_specs=[SMEM_SPEC] + [VMEM_SPEC] * (len(parts) + 2),
        out_specs=VMEM_SPEC,
        scratch_shapes=[pltpu.VMEM((WIDTH, ROWS), jnp.bfloat16), pltpu.VMEM((8, ROWS), jnp.float32)],
        compiler_params=pltpu.CompilerParams(vmem_limit_bytes=VMEM_LIMIT),
        name="tick",
    )(where, *parts, weights, mine)


def predict_kernel(where_ref, *refs):
    rows, blocks, taught, (out_ref, full) = refs[:8], refs[8:12], refs[12:14], refs[14:]
    segment = where_ref[1]
    for tau in range(TICKS):
        for ref, k, z, x, c in pieces(where_ref, rows[4 * tau : 4 * tau + 4]):
            at = pl.ds(feature_start(z, x, c), PIECE)
            full[at, tau * ROWS : (tau + 1) * ROWS] = ref[k * PIECE : (k + 1) * PIECE, :]
    total = jnp.zeros((COLS, TICKS * ROWS), jnp.float32)
    for ref, y in zip(blocks, y_labels(segment >> 1), strict=True):
        for i in range(2):
            for j in range(2):
                owner = (y ^ i) * 2 + ((segment & 1) ^ j)
                total += jnp.dot(
                    ref[(i * 2 + j) * COLS : (i * 2 + j + 1) * COLS, :],
                    full[pl.ds(pl.multiple_of(owner * BLOCK, BLOCK), BLOCK), :],
                    preferred_element_type=jnp.float32,
                )
    for tau in range(TICKS):
        difference = total[:, tau * ROWS : (tau + 1) * ROWS] - taught[tau][...].astype(jnp.float32)
        out_ref[tau * COLS : (tau + 1) * COLS, :] = difference.astype(jnp.bfloat16)


def predict(where, rows, blocks, taught):
    return pl.pallas_call(
        predict_kernel,
        out_shape=jax.ShapeDtypeStruct((TICKS * COLS, ROWS), jnp.bfloat16),
        in_specs=[SMEM_SPEC] + [VMEM_SPEC] * 14,
        out_specs=VMEM_SPEC,
        scratch_shapes=[pltpu.VMEM((WIDTH, TICKS * ROWS), jnp.bfloat16)],
        compiler_params=pltpu.CompilerParams(vmem_limit_bytes=VMEM_LIMIT),
        name="predict",
    )(where, *rows, *blocks, *taught)


def gradient_kernel(where_ref, *refs):
    diffs, parts, (keep_ref, send_ref, rows) = refs[:4], refs[4:8], refs[8:]
    segment = where_ref[1]
    for ref, k, z, x, c in pieces(where_ref, parts):
        y = z * 2 + (x >> 1)
        at = pl.ds(pl.multiple_of(((x & 1) * 2 + c) * PIECE, PIECE), PIECE)
        for tau in range(TICKS):
            source = pl.ds((k * TICKS + tau) * PIECE, PIECE)
            rows[y, at, tau * ROWS : (tau + 1) * ROWS] = ref[source, :]
    half = segment & 1
    for part, out_ref in ((half ^ 1, send_ref), (half, keep_ref)):
        total = jnp.zeros((COLS, BLOCK), jnp.float32)
        for ref, y in zip(diffs, y_labels(segment >> 1), strict=True):
            for i in range(2):
                both = [ref[(i * TICKS + tau) * COLS : (i * TICKS + tau + 1) * COLS, :] for tau in range(TICKS)]
                total += lax.dot_general(
                    jnp.concatenate(both, axis=1),
                    rows[y ^ i, pl.ds(pl.multiple_of(part * BLOCK, BLOCK), BLOCK), :],
                    (((1,), (1,)), ((), ())),
                    preferred_element_type=jnp.float32,
                )
        out_ref[...] = (total * (1.0 / (TICKS * ROWS))).astype(out_ref.dtype)


def gradient(where, diffs, parts):
    return pl.pallas_call(
        gradient_kernel,
        out_shape=(
            jax.ShapeDtypeStruct((COLS, BLOCK), jnp.float32),
            jax.ShapeDtypeStruct((COLS, BLOCK), jnp.bfloat16),
        ),
        in_specs=[SMEM_SPEC] + [VMEM_SPEC] * 8,
        out_specs=(VMEM_SPEC, VMEM_SPEC),
        scratch_shapes=[pltpu.VMEM((NY, 2 * BLOCK, TICKS * ROWS), jnp.bfloat16)],
        compiler_params=pltpu.CompilerParams(vmem_limit_bytes=VMEM_LIMIT),
        name="gradient",
    )(where, *diffs, *parts)


def on_device(entering, fresh_rows, norm_gain, segment_weight, projection, teacher_rows):
    t, segment = lax.axis_index("tensor"), lax.axis_index("segment")
    where = jnp.stack([t & 1, segment, t >> 3, (t >> 1) & 3]).astype(jnp.int32)
    weights = scaled_weights(segment_weight[0], norm_gain)
    teacher = teacher_rows[0].swapaxes(1, 2)
    entering_t, fresh_t = entering[0].T, fresh_rows[0].T

    mine_block = projection.T
    blocks = y_gather(stack(mine_block, zl_swap(mine_block)))
    taught = (to_next_segment(teacher[0], 0), teacher[1])

    out0 = tick(where, x_and_core(z_direct(entering_t)), weights, entering_t)

    moved = [to_next_segment(out0, mask) for mask in MASKS]
    earlier = x_and_core(stack(*moved))
    fresh = x_and_core(z_pairs(fresh_t))
    mine = jnp.where(segment == 0, fresh_t, moved[0])
    out1 = tick(where, earlier + fresh, weights, mine)

    turned = transposition(stack(moved[0], out1))
    later = x_and_core(z_direct(out1))
    difference = predict(where, earlier + later, blocks, taught)

    rows = x_and_core(z_pairs(turned))
    keep, send = gradient(where, y_gather(difference), rows)
    total = keep + zl_swap(send).astype(jnp.float32)
    return (out1.T[None], total.T)


def solution(mesh):
    return jax.shard_map(
        on_device,
        mesh=mesh,
        in_specs=(
            P("segment", None, "tensor"),
            P(None, None, "tensor"),
            P("segment", None),
            P("segment", "tensor", None),
            P("segment", "tensor"),
            P("segment", None, None, "tensor"),
        ),
        out_specs=(P("segment", None, "tensor"), P("segment", "tensor")),
        check_vma=False,
    )
```

```python
import jax
import jax.numpy as jnp
from jax import lax
from jax.experimental import pallas as pl
from jax.experimental.pallas import tpu as pltpu
from jax.sharding import PartitionSpec as P

EPSILON = 1e-05
TICKS = 2
NZ, NX, NC, NY = 4, 4, 2, 8
ROWS = 128
PIECE = 192
WIDTH = 6144
COLS = 288
BLOCK = 384
MASKS = (0, 1, 3, 2)
VMEM_LIMIT = 48 * 1024 * 1024
SMEM_SPEC = pl.BlockSpec(memory_space=pltpu.SMEM)
VMEM_SPEC = pl.BlockSpec(memory_space=pltpu.VMEM)


def t_index(z, x, c):
    return (z % NZ) * 8 + (x % NX) * 2 + c % NC


def all_t():
    return [(z, x, c) for z in range(NZ) for x in range(NX) for c in range(NC)]


def over_tensor(value, move):
    return lax.ppermute(value, "tensor", [(t_index(*p), t_index(*move(*p))) for p in all_t()])


def over_y(value, move):
    return lax.ppermute(
        value, "segment", [(y * 2 + zl, (move(y) % NY) * 2 + zl) for y in range(NY) for zl in range(2)]
    )


def z_swap(value, mask):
    return over_tensor(value, lambda z, x, c: (z ^ mask, x, c))


def x_swap(value, mask):
    return over_tensor(value, lambda z, x, c: (z, x ^ mask, c))


def core_swap(value):
    return over_tensor(value, lambda z, x, c: (z, x, c ^ 1))


def in_first_segment(value, move):
    pairs = [(t_index(*p), t_index(*move(*p))) for p in all_t()]
    return lax.ppermute(value, ("segment", "tensor"), pairs)


def first_segment_gather(value):
    two = stack(value, in_first_segment(value, lambda z, x, c: (z ^ 1, x, c)))
    four = stack(two, in_first_segment(two, lambda z, x, c: (z ^ 3, x, c)))
    near = stack(four, in_first_segment(four, lambda z, x, c: (z, x ^ 1, c)))
    far = in_first_segment(near, lambda z, x, c: (z, x ^ 3, c))
    return near, far, *[in_first_segment(v, lambda z, x, c: (z, x, c ^ 1)) for v in (near, far)]


def zl_swap(value):
    return lax.ppermute(value, "segment", [(i, i ^ 1) for i in range(16)])


def to_next_segment(value, mask):
    pairs = []
    for s in range(16):
        for z, x, c in all_t():
            pairs.append((s * 32 + t_index(z, x, c), ((s + 1) % 16) * 32 + t_index(z ^ mask, x, c)))
    return lax.ppermute(value, ("segment", "tensor"), pairs)


def transposition(value):
    pairs = []
    for yy in range(NY):
        for zl in range(2):
            for z, x, c in all_t():
                y = z * 2 + (x >> 1)
                there = t_index(yy >> 1, (yy & 1) * 2 + (x & 1), c)
                pairs.append(((yy * 2 + zl) * 32 + t_index(z, x, c), (y * 2 + zl) * 32 + there))
    return lax.ppermute(value, ("segment", "tensor"), pairs)


def stack(*values):
    return jnp.concatenate(values, axis=0)


def z_direct(value):
    return stack(value, *[z_swap(value, mask) for mask in MASKS[1:]])


def other_neighbour(y):
    return y - 1 if y % 2 == 0 else y + 1


def y_labels(y):
    def other(v):
        return lax.rem(v + jnp.where(lax.rem(v, 2) == 0, NY - 1, 1), NY)

    away = lax.rem(y + jnp.where(lax.rem(y, 2) == 0, NY - 2, 2), NY)
    return y, other(y), other(y ^ 1), other(away)


def scaled_weights(weights, gain):
    return (weights.astype(jnp.float32) * gain).astype(jnp.bfloat16)


def pieces(where_ref, parts):
    core, z_mine, x_mine = where_ref[0], where_ref[2], where_ref[3]
    for ref, far, c in zip(parts, (0, 1, 0, 1), (core, core, core ^ 1, core ^ 1), strict=True):
        for i in range(2):
            for j in range(NZ):
                yield ref, i * NZ + j, z_mine ^ MASKS[j], x_mine ^ MASKS[2 * far + i], c


def feature_start(z, x, c):
    return pl.multiple_of((z * 8 + x * 2 + c) * PIECE, PIECE)


def tick_kernel(where_ref, *refs):
    parts, (weight_ref, mine_ref, out_ref, full, square) = refs[:-5], refs[-5:]

    def fill(four):
        square[...] = jnp.zeros((8, ROWS), jnp.float32)
        for ref, k, z, x, c in pieces(where_ref, four):
            piece = ref[k * PIECE : (k + 1) * PIECE, :]
            full[pl.ds(feature_start(z, x, c), PIECE), :] = piece
            wide = piece.astype(jnp.float32)
            square[...] += jnp.sum((wide * wide).reshape(PIECE // 8, 8, ROWS), axis=0)

    if len(parts) == 4:
        fill(parts)
    else:
        first = where_ref[1] == 0

        @pl.when(first)
        def _():
            fill(parts[4:])

        @pl.when(jnp.logical_not(first))
        def _():
            fill(parts[:4])

    mean_square = jnp.sum(square[...], axis=0, keepdims=True) * (1.0 / WIDTH)
    scale = lax.rsqrt(mean_square + EPSILON)
    hidden = jnp.dot(weight_ref[...], full[...], preferred_element_type=jnp.float32) * scale
    silu = hidden / (1.0 + jnp.exp(-hidden))
    out_ref[...] = (mine_ref[...].astype(jnp.float32) + silu).astype(jnp.bfloat16)


def tick(where, parts, weights, mine):
    return pl.pallas_call(
        tick_kernel,
        out_shape=jax.ShapeDtypeStruct((PIECE, ROWS), jnp.bfloat16),
        in_specs=[SMEM_SPEC] + [VMEM_SPEC] * (len(parts) + 2),
        out_specs=VMEM_SPEC,
        scratch_shapes=[pltpu.VMEM((WIDTH, ROWS), jnp.bfloat16), pltpu.VMEM((8, ROWS), jnp.float32)],
        compiler_params=pltpu.CompilerParams(vmem_limit_bytes=VMEM_LIMIT),
        name="tick",
    )(where, *parts, weights, mine)


def predict_kernel(where_ref, *refs):
    rows, blocks, taught, (out_ref, full) = refs[:8], refs[8:12], refs[12:14], refs[14:]
    segment = where_ref[1]
    for tau in range(TICKS):
        for ref, k, z, x, c in pieces(where_ref, rows[4 * tau : 4 * tau + 4]):
            at = pl.ds(feature_start(z, x, c), PIECE)
            full[at, tau * ROWS : (tau + 1) * ROWS] = ref[k * PIECE : (k + 1) * PIECE, :]
    total = jnp.zeros((COLS, TICKS * ROWS), jnp.float32)
    for ref, y in zip(blocks, y_labels(segment >> 1), strict=True):
        for i in range(2):
            for j in range(2):
                owner = (y ^ i) * 2 + ((segment & 1) ^ j)
                total += jnp.dot(
                    ref[(i * 2 + j) * COLS : (i * 2 + j + 1) * COLS, :],
                    full[pl.ds(pl.multiple_of(owner * BLOCK, BLOCK), BLOCK), :],
                    preferred_element_type=jnp.float32,
                )
    for tau in range(TICKS):
        difference = total[:, tau * ROWS : (tau + 1) * ROWS] - taught[tau][...].astype(jnp.float32)
        out_ref[tau * COLS : (tau + 1) * COLS, :] = difference.astype(jnp.bfloat16)


def predict(where, rows, blocks, taught):
    return pl.pallas_call(
        predict_kernel,
        out_shape=jax.ShapeDtypeStruct((TICKS * COLS, ROWS), jnp.bfloat16),
        in_specs=[SMEM_SPEC] + [VMEM_SPEC] * 14,
        out_specs=VMEM_SPEC,
        scratch_shapes=[pltpu.VMEM((WIDTH, TICKS * ROWS), jnp.bfloat16)],
        compiler_params=pltpu.CompilerParams(vmem_limit_bytes=VMEM_LIMIT),
        name="predict",
    )(where, *rows, *blocks, *taught)


def gradient_kernel(where_ref, *refs):
    diffs, parts, (keep_ref, send_ref, rows) = refs[:4], refs[4:8], refs[8:]
    segment = where_ref[1]
    for ref, k, z, x, c in pieces(where_ref, parts):
        y = z * 2 + (x >> 1)
        at = pl.ds(pl.multiple_of(((x & 1) * 2 + c) * PIECE, PIECE), PIECE)
        for tau in range(TICKS):
            source = pl.ds((k * TICKS + tau) * PIECE, PIECE)
            rows[y, at, tau * ROWS : (tau + 1) * ROWS] = ref[source, :]
    half = segment & 1
    for part, out_ref in ((half ^ 1, send_ref), (half, keep_ref)):
        total = jnp.zeros((COLS, BLOCK), jnp.float32)
        for ref, y in zip(diffs, y_labels(segment >> 1), strict=True):
            for i in range(2):
                both = [ref[(i * TICKS + tau) * COLS : (i * TICKS + tau + 1) * COLS, :] for tau in range(TICKS)]
                total += lax.dot_general(
                    jnp.concatenate(both, axis=1),
                    rows[y ^ i, pl.ds(pl.multiple_of(part * BLOCK, BLOCK), BLOCK), :],
                    (((1,), (1,)), ((), ())),
                    preferred_element_type=jnp.float32,
                )
        out_ref[...] = (total * (1.0 / (TICKS * ROWS))).astype(out_ref.dtype)


def gradient(where, diffs, parts):
    return pl.pallas_call(
        gradient_kernel,
        out_shape=(
            jax.ShapeDtypeStruct((COLS, BLOCK), jnp.float32),
            jax.ShapeDtypeStruct((COLS, BLOCK), jnp.bfloat16),
        ),
        in_specs=[SMEM_SPEC] + [VMEM_SPEC] * 8,
        out_specs=(VMEM_SPEC, VMEM_SPEC),
        scratch_shapes=[pltpu.VMEM((NY, 2 * BLOCK, TICKS * ROWS), jnp.bfloat16)],
        compiler_params=pltpu.CompilerParams(vmem_limit_bytes=VMEM_LIMIT),
        name="gradient",
    )(where, *diffs, *parts)


def together(*values):
    return lax.optimization_barrier(values)


def on_device(entering, fresh_rows, norm_gain, segment_weight, projection, teacher_rows):
    t, segment = lax.axis_index("tensor"), lax.axis_index("segment")
    where = jnp.stack([t & 1, segment, t >> 3, (t >> 1) & 3]).astype(jnp.int32)
    weights = scaled_weights(segment_weight[0], norm_gain)
    teacher = teacher_rows[0].swapaxes(1, 2)
    entering_t, fresh_t = entering[0].T, fresh_rows[0].T

    mine_block = projection.T
    unit = stack(mine_block, zl_swap(mine_block))

    both_z = z_direct(entering_t)
    both_z, unit, teacher0 = together(both_z, unit, teacher[0])
    unit_a = over_y(unit, lambda y: y ^ 1)
    near = stack(both_z, x_swap(both_z, 1))
    taught0 = to_next_segment(teacher0, 0)
    near, unit_a, fresh_t = together(near, unit_a, fresh_t)
    pair = stack(unit, unit_a)
    far = x_swap(near, 3)
    second = over_y(pair, other_neighbour)
    parts = near, far, core_swap(near), core_swap(far)
    out0 = tick(where, parts, weights, entering_t)
    out0, taught0 = together(out0, taught0)

    moved = [to_next_segment(out0, mask) for mask in MASKS]
    earlier_z = stack(*moved)
    earlier_z, second = together(earlier_z, second)
    near = stack(earlier_z, x_swap(earlier_z, 1))
    third = over_y(second, lambda y: y ^ 1)
    fourth = over_y(second, lambda y: y + 2 if y % 2 == 0 else y - 2)
    blocks = pair, second, third, fourth
    far = x_swap(near, 3)
    earlier = near, far, core_swap(near), core_swap(far)
    fresh = first_segment_gather(fresh_t)
    mine = jnp.where(segment == 0, fresh_t, moved[0])
    out1 = tick(where, earlier + fresh, weights, mine)

    turned = transposition(stack(moved[0], out1))
    later_z = z_direct(out1)
    near = stack(later_z, x_swap(later_z, 1))
    near, turned = together(near, turned)
    far = x_swap(near, 3)
    two = stack(turned, z_swap(turned, 1))
    far, two = together(far, two)
    later = near, far, core_swap(near), core_swap(far)
    rows_z = stack(two, z_swap(two, 3))
    difference = predict(where, earlier + later, blocks, (taught0, teacher[1]))

    rows_z, _ = together(rows_z, difference)
    pair = stack(difference, over_y(difference, lambda y: y ^ 1))
    near = stack(rows_z, x_swap(rows_z, 1))
    near, _ = together(near, pair)
    second = over_y(pair, other_neighbour)
    far = x_swap(near, 3)
    third = over_y(second, lambda y: y ^ 1)
    fourth = over_y(second, lambda y: y + 2 if y % 2 == 0 else y - 2)
    rows = near, far, core_swap(near), core_swap(together(far, second)[0])
    keep, send = gradient(where, (pair, second, third, fourth), rows)
    total = keep + zl_swap(send).astype(jnp.float32)
    return (out1.T[None], total.T)


def solution(mesh):
    return jax.shard_map(
        on_device,
        mesh=mesh,
        in_specs=(
            P("segment", None, "tensor"),
            P(None, None, "tensor"),
            P("segment", None),
            P("segment", "tensor", None),
            P("segment", "tensor"),
            P("segment", None, None, "tensor"),
        ),
        out_specs=(P("segment", None, "tensor"), P("segment", "tensor")),
        check_vma=False,
    )
```

```python
import jax
import jax.numpy as jnp
from jax import lax
from jax.experimental import pallas as pl
from jax.experimental.pallas import tpu as pltpu
from jax.sharding import PartitionSpec as P

EPSILON = 1e-05
TICKS = 2
NZ, NX, NC, NY = 4, 4, 2, 8
ROWS = 128
PIECE = 192
WIDTH = 6144
COLS = 288
BLOCK = 384
MASKS = (0, 1, 3, 2)
VMEM_LIMIT = 24 * 1024 * 1024
SMEM_SPEC = pl.BlockSpec(memory_space=pltpu.SMEM)
VMEM_SPEC = pl.BlockSpec(memory_space=pltpu.VMEM)


def t_index(z, x, c):
    return (z % NZ) * 8 + (x % NX) * 2 + c % NC


def all_t():
    return [(z, x, c) for z in range(NZ) for x in range(NX) for c in range(NC)]


X_GROUPS = [[t_index(z, x, c) for x in range(NX)] for z in range(NZ) for c in range(NC)]


def over_tensor(value, move):
    return lax.ppermute(value, "tensor", [(t_index(*p), t_index(*move(*p))) for p in all_t()])


def over_y(value, move):
    return lax.ppermute(
        value, "segment", [(y * 2 + zl, (move(y) % NY) * 2 + zl) for y in range(NY) for zl in range(2)]
    )


def z_swap(value, mask):
    return over_tensor(value, lambda z, x, c: (z ^ mask, x, c))


def core_swap(value):
    return over_tensor(value, lambda z, x, c: (z, x, c ^ 1))


def zl_swap(value):
    return lax.ppermute(value, "segment", [(i, i ^ 1) for i in range(16)])


def in_first_segment(value, move):
    pairs = [(t_index(*p), t_index(*move(*p))) for p in all_t()]
    return lax.ppermute(value, ("segment", "tensor"), pairs)


def first_segment_x_and_core(value):
    near = stack(value, in_first_segment(value, lambda z, x, c: (z, x ^ 1, c)))
    far = in_first_segment(near, lambda z, x, c: (z, x ^ 3, c))
    return near, far, *[in_first_segment(v, lambda z, x, c: (z, x, c ^ 1)) for v in (near, far)]


def to_next_segment(value, mask):
    pairs = []
    for s in range(16):
        for z, x, c in all_t():
            pairs.append((s * 32 + t_index(z, x, c), ((s + 1) % 16) * 32 + t_index(z ^ mask, x, c)))
    return lax.ppermute(value, ("segment", "tensor"), pairs)


def transposition(value):
    pairs = []
    for yy in range(NY):
        for zl in range(2):
            for z, x, c in all_t():
                y = z * 2 + (x >> 1)
                there = t_index(yy >> 1, (yy & 1) * 2 + (x & 1), c)
                pairs.append(((yy * 2 + zl) * 32 + t_index(z, x, c), (y * 2 + zl) * 32 + there))
    return lax.ppermute(value, ("segment", "tensor"), pairs)


def stack(*values):
    return jnp.concatenate(values, axis=0)


def together(*values):
    return lax.optimization_barrier(values)


def z_direct(value):
    return stack(value, *[z_swap(value, mask) for mask in MASKS[1:]])


def x_and_core(value):
    own = lax.all_gather(value, "tensor", axis=0, tiled=True, axis_index_groups=X_GROUPS)
    return own, core_swap(own)


def other_neighbour(y):
    return y - 1 if y % 2 == 0 else y + 1


def y_labels(y):
    def other(v):
        return lax.rem(v + jnp.where(lax.rem(v, 2) == 0, NY - 1, 1), NY)

    away = lax.rem(y + jnp.where(lax.rem(y, 2) == 0, NY - 2, 2), NY)
    return y, other(y), other(y ^ 1), other(away)


def scaled_weights(weights, gain):
    return (weights.astype(jnp.float32) * gain).astype(jnp.bfloat16)


def pieces(where_ref, parts):
    core, z_mine, x_mine = where_ref[0], where_ref[2], where_ref[3]
    if len(parts) == 2:
        for ref, c in zip(parts, (core, core ^ 1), strict=True):
            for i in range(NX):
                for j in range(NZ):
                    yield ref, i * NZ + j, z_mine ^ MASKS[j], i, c
    else:
        for ref, far, c in zip(parts, (0, 1, 0, 1), (core, core, core ^ 1, core ^ 1), strict=True):
            for i in range(2):
                for j in range(NZ):
                    yield ref, i * NZ + j, z_mine ^ MASKS[j], x_mine ^ MASKS[2 * far + i], c


def feature_start(z, x, c):
    return pl.multiple_of((z * 8 + x * 2 + c) * PIECE, PIECE)


def tick_kernel(where_ref, own_ref, other_ref, weight_ref, mine_ref, out_ref, full):
    square = jnp.zeros((8, ROWS), jnp.float32)
    for ref, k, z, x, c in pieces(where_ref, (own_ref, other_ref)):
        piece = ref[k * PIECE : (k + 1) * PIECE, :]
        full[pl.ds(feature_start(z, x, c), PIECE), :] = piece
        wide = piece.astype(jnp.float32)
        square += jnp.sum((wide * wide).reshape(PIECE // 8, 8, ROWS), axis=0)
    mean_square = jnp.sum(square, axis=0, keepdims=True) * (1.0 / WIDTH)
    scale = lax.rsqrt(mean_square + EPSILON)
    hidden = jnp.dot(weight_ref[...], full[...], preferred_element_type=jnp.float32) * scale
    silu = hidden / (1.0 + jnp.exp(-hidden))
    out_ref[...] = (mine_ref[...].astype(jnp.float32) + silu).astype(jnp.bfloat16)


def tick(where, parts, weights, mine):
    return pl.pallas_call(
        tick_kernel,
        out_shape=jax.ShapeDtypeStruct((PIECE, ROWS), jnp.bfloat16),
        in_specs=[SMEM_SPEC] + [VMEM_SPEC] * 4,
        out_specs=VMEM_SPEC,
        scratch_shapes=[pltpu.VMEM((WIDTH, ROWS), jnp.bfloat16)],
        compiler_params=pltpu.CompilerParams(vmem_limit_bytes=VMEM_LIMIT),
        name="tick",
    )(where, *parts, weights, mine)


def predict_kernel(where_ref, *refs):
    earlier, wrapped, later = refs[:2], refs[2:6], refs[6:8]
    block_ref, taught0_ref, taught1_ref, out_ref, full = refs[8:]

    def fill(parts, tau):
        for ref, k, z, x, c in pieces(where_ref, parts):
            at = pl.ds(feature_start(z, x, c), PIECE)
            full[at, tau * ROWS : (tau + 1) * ROWS] = ref[k * PIECE : (k + 1) * PIECE, :]

    first = where_ref[1] == 0

    @pl.when(first)
    def _():
        fill(wrapped, 0)

    @pl.when(jnp.logical_not(first))
    def _():
        fill(earlier, 0)

    fill(later, 1)
    total = jnp.zeros((COLS, TICKS * ROWS), jnp.float32)
    for s in range(16):
        total += jnp.dot(
            block_ref[s * COLS : (s + 1) * COLS, :],
            full[s * BLOCK : (s + 1) * BLOCK, :],
            preferred_element_type=jnp.float32,
        )
    for tau, taught in enumerate((taught0_ref[0], taught1_ref[1])):
        difference = total[:, tau * ROWS : (tau + 1) * ROWS] - taught.astype(jnp.float32)
        out_ref[tau * COLS : (tau + 1) * COLS, :] = difference.astype(jnp.bfloat16)


def predict(where, rows, blocks, taught):
    return pl.pallas_call(
        predict_kernel,
        out_shape=jax.ShapeDtypeStruct((TICKS * COLS, ROWS), jnp.bfloat16),
        in_specs=[SMEM_SPEC] + [VMEM_SPEC] * 11,
        out_specs=VMEM_SPEC,
        scratch_shapes=[pltpu.VMEM((WIDTH, TICKS * ROWS), jnp.bfloat16)],
        compiler_params=pltpu.CompilerParams(vmem_limit_bytes=VMEM_LIMIT),
        name="predict",
    )(where, *rows, blocks, *taught)


def gradient_kernel(where_ref, *refs):
    diffs, (rows_ref, keep_ref, send_ref, rows) = refs[:4], refs[4:]
    segment = where_ref[1]
    for z, x, c in all_t():
        start = ((x & 1) * 2 + c) * PIECE
        for tau in range(TICKS):
            source = (t_index(z, x, c) * TICKS + tau) * PIECE
            columns = slice(tau * ROWS, (tau + 1) * ROWS)
            rows[z * 2 + (x >> 1), start : start + PIECE, columns] = rows_ref[source : source + PIECE, :]
    half = segment & 1
    for part, out_ref in ((half ^ 1, send_ref), (half, keep_ref)):
        total = jnp.zeros((COLS, BLOCK), jnp.float32)
        for ref, y in zip(diffs, y_labels(segment >> 1), strict=True):
            for i in range(2):
                both = [ref[(i * TICKS + tau) * COLS : (i * TICKS + tau + 1) * COLS, :] for tau in range(TICKS)]
                total += lax.dot_general(
                    jnp.concatenate(both, axis=1),
                    rows[y ^ i, pl.ds(pl.multiple_of(part * BLOCK, BLOCK), BLOCK), :],
                    (((1,), (1,)), ((), ())),
                    preferred_element_type=jnp.float32,
                )
        out_ref[...] = (total * (1.0 / (TICKS * ROWS))).astype(out_ref.dtype)


def gradient(where, diffs, rows):
    return pl.pallas_call(
        gradient_kernel,
        out_shape=(
            jax.ShapeDtypeStruct((COLS, BLOCK), jnp.float32),
            jax.ShapeDtypeStruct((COLS, BLOCK), jnp.bfloat16),
        ),
        in_specs=[SMEM_SPEC] + [VMEM_SPEC] * 5,
        out_specs=(VMEM_SPEC, VMEM_SPEC),
        scratch_shapes=[pltpu.VMEM((NY, 2 * BLOCK, TICKS * ROWS), jnp.bfloat16)],
        compiler_params=pltpu.CompilerParams(vmem_limit_bytes=VMEM_LIMIT),
        name="gradient",
    )(where, *diffs, rows)


def on_device(entering, fresh_rows, norm_gain, segment_weight, projection, teacher_rows):
    t, segment = lax.axis_index("tensor"), lax.axis_index("segment")
    where = jnp.stack([t & 1, segment, t >> 3, (t >> 1) & 3]).astype(jnp.int32)
    weights = scaled_weights(segment_weight[0], norm_gain)
    teacher = teacher_rows[0].swapaxes(1, 2)
    entering_t, fresh_t = entering[0].T, fresh_rows[0].T

    blocks = lax.all_gather(projection.T, "segment", axis=0, tiled=True)
    taught0 = to_next_segment(teacher, 0)

    start = stack(entering_t, fresh_t)
    got = [start] + [z_swap(start, mask) for mask in MASKS[1:]]
    fresh_z = stack(*[v[PIECE:] for v in got])
    out0 = tick(where, x_and_core(stack(*[v[:PIECE] for v in got])), weights, entering_t)

    out0, taught0 = together(out0, taught0)
    moved = [to_next_segment(out0, mask) for mask in MASKS]
    moved_z = stack(*moved)
    first = segment == 0
    earlier = x_and_core(jnp.where(first, fresh_z, moved_z))
    wrapped = first_segment_x_and_core(together(moved_z, earlier[0])[0])
    out1 = tick(where, earlier, weights, jnp.where(first, fresh_t, moved[0]))

    turned = transposition(stack(moved[0], out1))
    later_z = z_direct(out1)
    turned, _ = together(turned, later_z)
    rows = lax.all_gather(turned, "tensor", axis=0, tiled=True)
    later = x_and_core(later_z)
    difference = predict(where, earlier + wrapped + later, blocks, (taught0, teacher))

    pair = stack(difference, over_y(difference, lambda y: y ^ 1))
    second = over_y(pair, other_neighbour)
    third = over_y(second, lambda y: y ^ 1)
    fourth = over_y(second, lambda y: y + 2 if y % 2 == 0 else y - 2)
    keep, send = gradient(where, (pair, second, third, fourth), rows)
    total = keep + zl_swap(send).astype(jnp.float32)
    return (out1.T[None], total.T)


def solution(mesh):
    return jax.shard_map(
        on_device,
        mesh=mesh,
        in_specs=(
            P("segment", None, "tensor"),
            P(None, None, "tensor"),
            P("segment", None),
            P("segment", "tensor", None),
            P("segment", "tensor"),
            P("segment", None, None, "tensor"),
        ),
        out_specs=(P("segment", None, "tensor"), P("segment", "tensor")),
        check_vma=False,
    )
```

```python
import jax
import jax.numpy as jnp
from jax import lax
from jax.experimental import pallas as pl
from jax.experimental.pallas import tpu as pltpu
from jax.sharding import PartitionSpec as P

EPSILON = 1e-05
TICKS = 2
NZ, NX, NC, NY = 4, 4, 2, 8
ROWS = 128
PIECE = 192
WIDTH = 6144
COLS = 288
BLOCK = 384
COLUMN = 768
RIDE = 960
VMEM_LIMIT = 32 * 1024 * 1024
SMEM_SPEC = pl.BlockSpec(memory_space=pltpu.SMEM)
VMEM_SPEC = pl.BlockSpec(memory_space=pltpu.VMEM)


def t_index(z, x, c):
    return (z % NZ) * 8 + (x % NX) * 2 + c % NC


def all_t():
    return [(z, x, c) for z in range(NZ) for x in range(NX) for c in range(NC)]


Z_GROUPS = [[t_index(z, x, c) for z in range(NZ)] for x in range(NX) for c in range(NC)]
Y_GROUPS = [[y * 2 + zl for y in range(NY)] for zl in range(2)]
X_GROUPS = [[t_index(z, x, c) for x in range(NX)] for z in range(NZ) for c in range(NC)]


def over_tensor(value, move):
    return lax.ppermute(value, "tensor", [(t_index(*p), t_index(*move(*p))) for p in all_t()])


def over_y(value, move):
    return lax.ppermute(
        value, "segment", [(y * 2 + zl, (move(y) % NY) * 2 + zl) for y in range(NY) for zl in range(2)]
    )


def core_swap(value):
    return over_tensor(value, lambda z, x, c: (z, x, c ^ 1))


def zl_swap(value):
    return lax.ppermute(value, "segment", [(i, i ^ 1) for i in range(16)])


def transposition(value):
    pairs = []
    for yy in range(NY):
        for zl in range(2):
            for z, x, c in all_t():
                y = z * 2 + (x >> 1)
                there = t_index(yy >> 1, (yy & 1) * 2 + (x & 1), c)
                pairs.append(((yy * 2 + zl) * 32 + t_index(z, x, c), (y * 2 + zl) * 32 + there))
    return lax.ppermute(value, ("segment", "tensor"), pairs)


def stack(*values):
    return jnp.concatenate(values, axis=0)


def together(*values):
    return lax.optimization_barrier(values)


def gather(value, axis, groups):
    return lax.all_gather(value, axis, axis=0, tiled=True, axis_index_groups=groups)


def z_gather(value):
    return gather(value, "tensor", Z_GROUPS)


def x_gather(value):
    return gather(value, "tensor", X_GROUPS)


def whole(shape):
    return pl.BlockSpec(shape, lambda i: (0,) * len(shape))


def other_neighbour(y):
    return y - 1 if y % 2 == 0 else y + 1


def y_labels(y):
    def other(v):
        return lax.rem(v + jnp.where(lax.rem(v, 2) == 0, NY - 1, 1), NY)

    away = lax.rem(y + jnp.where(lax.rem(y, 2) == 0, NY - 2, 2), NY)
    return y, other(y), other(y ^ 1), other(away)


def scaled_weights(weights, gain):
    return (weights.astype(jnp.float32) * gain).astype(jnp.bfloat16)


def feature_start(z, x, c):
    return pl.multiple_of((z * 8 + x * 2 + c) * PIECE, PIECE)


def hidden_rows(where_ref, own_ref, other_ref, weight_ref, mine_ref, full):
    core = where_ref[0]
    stride = own_ref.shape[0] // NX
    square = jnp.zeros((8, ROWS), jnp.float32)
    for ref, c in ((own_ref, core), (other_ref, core ^ 1)):
        for x in range(NX):
            for z in range(NZ):
                source = x * stride + z * PIECE
                piece = ref[source : source + PIECE, :]
                full[pl.ds(feature_start(z, x, c), PIECE), :] = piece
                wide = piece.astype(jnp.float32)
                square += jnp.sum((wide * wide).reshape(PIECE // 8, 8, ROWS), axis=0)
    mean_square = jnp.sum(square, axis=0, keepdims=True) * (1.0 / WIDTH)
    scale = lax.rsqrt(mean_square + EPSILON)
    hidden = jnp.dot(weight_ref[...], full[...], preferred_element_type=jnp.float32) * scale
    silu = hidden / (1.0 + jnp.exp(-hidden))
    return (mine_ref[...].astype(jnp.float32) + silu).astype(jnp.bfloat16)


def first_tick_kernel(where_ref, own_ref, other_ref, weight_ref, mine_ref, out_ref, full):
    out_ref[...] = hidden_rows(where_ref, own_ref, other_ref, weight_ref, mine_ref, full)


def second_tick_kernel(
    where_ref, own_ref, other_ref, weight_ref, mine_ref, before_ref, out_ref, both_ref, next_ref, full
):
    out = hidden_rows(where_ref, own_ref, other_ref, weight_ref, mine_ref, full)
    out_ref[...] = out
    both_ref[:PIECE, :] = before_ref[...]
    both_ref[PIECE:, :] = out
    next_ref[:PIECE, :] = out
    for x in range(NX):
        source = x * RIDE + COLUMN
        next_ref[(x + 1) * PIECE : (x + 2) * PIECE, :] = own_ref[source : source + PIECE, :]


def tick(kernel, out_rows, *operands):
    return pl.pallas_call(
        kernel,
        out_shape=[jax.ShapeDtypeStruct((rows, ROWS), jnp.bfloat16) for rows in out_rows],
        in_specs=[SMEM_SPEC] + [VMEM_SPEC] * (len(operands) - 1),
        out_specs=[VMEM_SPEC] * len(out_rows),
        scratch_shapes=[pltpu.VMEM((WIDTH, ROWS), jnp.bfloat16)],
        compiler_params=pltpu.CompilerParams(vmem_limit_bytes=VMEM_LIMIT),
        name="tick",
    )(*operands)


def predict_kernel(
    where_ref, first_own_ref, first_other_ref, own_ref, other_ref, block_ref, teacher_ref, out_ref, full
):
    core, segment = where_ref[0], where_ref[1]
    for ref, c in ((first_own_ref, core), (first_other_ref, core ^ 1)):
        for z in range(NZ):
            for x in range(NX):
                source = z * RIDE + (x + 1) * PIECE
                full[pl.ds(feature_start(z, x, c), PIECE), :ROWS] = ref[source : source + PIECE, :]
    for ref, c in ((own_ref, core), (other_ref, core ^ 1)):
        for x in range(NX):
            for z in range(NZ):
                source = (x * NZ + z) * PIECE
                full[pl.ds(feature_start(z, x, c), PIECE), ROWS:] = ref[source : source + PIECE, :]
    total = jnp.zeros((COLS, TICKS * ROWS), jnp.float32)
    for y in range(NY):
        for j in range(2):
            owner = y * 2 + ((segment & 1) ^ j)
            total += jnp.dot(
                block_ref[(y * 2 + j) * COLS : (y * 2 + j + 1) * COLS, :],
                full[pl.ds(pl.multiple_of(owner * BLOCK, BLOCK), BLOCK), :],
                preferred_element_type=jnp.float32,
            )
    for tau in range(TICKS):
        difference = total[:, tau * ROWS : (tau + 1) * ROWS] - teacher_ref[tau].astype(jnp.float32)
        out_ref[tau * COLS : (tau + 1) * COLS, :] = difference.astype(jnp.bfloat16)


def predict(where, *operands):
    return pl.pallas_call(
        predict_kernel,
        grid=(1,),
        out_shape=jax.ShapeDtypeStruct((TICKS * COLS, ROWS), jnp.bfloat16),
        in_specs=[SMEM_SPEC] + [whole(v.shape) for v in operands],
        out_specs=whole((TICKS * COLS, ROWS)),
        scratch_shapes=[pltpu.VMEM((WIDTH, TICKS * ROWS), jnp.bfloat16)],
        compiler_params=pltpu.CompilerParams(vmem_limit_bytes=VMEM_LIMIT),
        name="predict",
    )(where, *operands)


def gradient_kernel(where_ref, *refs):
    diffs, (rows_ref, keep_ref, send_ref, rows) = refs[:4], refs[4:]
    segment = where_ref[1]
    for z, x, c in all_t():
        start = ((x & 1) * 2 + c) * PIECE
        for tau in range(TICKS):
            source = (t_index(z, x, c) * TICKS + tau) * PIECE
            columns = slice(tau * ROWS, (tau + 1) * ROWS)
            rows[z * 2 + (x >> 1), start : start + PIECE, columns] = rows_ref[source : source + PIECE, :]
    half = segment & 1
    for part, out_ref in ((half ^ 1, send_ref), (half, keep_ref)):
        total = jnp.zeros((COLS, BLOCK), jnp.float32)
        for ref, y in zip(diffs, y_labels(segment >> 1), strict=True):
            for i in range(2):
                both = [ref[(i * TICKS + tau) * COLS : (i * TICKS + tau + 1) * COLS, :] for tau in range(TICKS)]
                total += lax.dot_general(
                    jnp.concatenate(both, axis=1),
                    rows[y ^ i, pl.ds(pl.multiple_of(part * BLOCK, BLOCK), BLOCK), :],
                    (((1,), (1,)), ((), ())),
                    preferred_element_type=jnp.float32,
                )
        out_ref[...] = (total * (1.0 / (TICKS * ROWS))).astype(out_ref.dtype)


def gradient(where, diffs, rows):
    return pl.pallas_call(
        gradient_kernel,
        out_shape=(
            jax.ShapeDtypeStruct((COLS, BLOCK), jnp.float32),
            jax.ShapeDtypeStruct((COLS, BLOCK), jnp.bfloat16),
        ),
        grid=(1,),
        in_specs=[SMEM_SPEC] + [whole(v.shape) for v in (*diffs, rows)],
        out_specs=(whole((COLS, BLOCK)), whole((COLS, BLOCK))),
        scratch_shapes=[pltpu.VMEM((NY, 2 * BLOCK, TICKS * ROWS), jnp.bfloat16)],
        compiler_params=pltpu.CompilerParams(vmem_limit_bytes=VMEM_LIMIT),
        name="gradient",
    )(where, *diffs, rows)


def on_device(entering, fresh_rows, norm_gain, segment_weight, projection, teacher_rows):
    t, segment = lax.axis_index("tensor"), lax.axis_index("segment")
    where = jnp.stack([t & 1, segment]).astype(jnp.int32)
    weights = scaled_weights(segment_weight[0], norm_gain)
    teacher = teacher_rows[0].swapaxes(1, 2)
    entering_t, fresh_t = entering[0].T, fresh_rows[0].T

    mine_block = projection.T
    first = z_gather(entering_t)
    other_block, first = together(zl_swap(mine_block), first)
    blocks = gather(stack(mine_block, other_block), "segment", Y_GROUPS)
    own = x_gather(first)
    (out0,) = tick(first_tick_kernel, (PIECE,), where, own, core_swap(own), weights, entering_t)

    shifted = lax.ppermute(out0, "segment", [(i, i + 1) for i in range(15)])
    mine = jnp.where(segment == 0, fresh_t, shifted)
    own = x_gather(stack(z_gather(mine), out0))
    out1, both, following = tick(
        second_tick_kernel, (PIECE, 2 * PIECE, RIDE), where, own, core_swap(own), weights, mine, out0
    )

    turned = transposition(both)
    first_own = z_gather(following)
    turned, blocks, first_own = together(turned, blocks, first_own)
    rows = lax.all_gather(turned, "tensor", axis=0, tiled=True)
    own = x_gather(first_own.reshape(NZ, RIDE, ROWS)[:, :PIECE].reshape(COLUMN, ROWS))
    difference = predict(where, first_own, core_swap(first_own), own, core_swap(own), blocks, teacher)

    pair = stack(difference, over_y(difference, lambda y: y ^ 1))
    second = over_y(pair, other_neighbour)
    third = over_y(second, lambda y: y ^ 1)
    fourth = over_y(second, lambda y: y + 2 if y % 2 == 0 else y - 2)
    keep, send = gradient(where, (pair, second, third, fourth), rows)
    total = keep + zl_swap(send).astype(jnp.float32)
    return (out1.T[None], total.T)


def solution(mesh):
    return jax.shard_map(
        on_device,
        mesh=mesh,
        in_specs=(
            P("segment", None, "tensor"),
            P(None, None, "tensor"),
            P("segment", None),
            P("segment", "tensor", None),
            P("segment", "tensor"),
            P("segment", None, None, "tensor"),
        ),
        out_specs=(P("segment", None, "tensor"), P("segment", "tensor")),
        check_vma=False,
    )
```

```python
import jax
import jax.numpy as jnp
from jax import lax
from jax.experimental import pallas as pl
from jax.experimental.pallas import tpu as pltpu
from jax.sharding import PartitionSpec as P

EPSILON = 1e-05
TICKS = 2
NZ, NX, NC, NY = 4, 4, 2, 8
ROWS = 128
PIECE = 192
WIDTH = 6144
COLS = 288
BLOCK = 384
COLUMN = 768
RIDE = 960
VMEM_LIMIT = 32 * 1024 * 1024
SMEM_SPEC = pl.BlockSpec(memory_space=pltpu.SMEM)
VMEM_SPEC = pl.BlockSpec(memory_space=pltpu.VMEM)


def t_index(z, x, c):
    return (z % NZ) * 8 + (x % NX) * 2 + c % NC


def all_t():
    return [(z, x, c) for z in range(NZ) for x in range(NX) for c in range(NC)]


Z_GROUPS = [[t_index(z, x, c) for z in range(NZ)] for x in range(NX) for c in range(NC)]
SECOND_Y_GROUPS = [[(2 * i + p) * 2 + zl for i in range(NY // 2)] for p in range(2) for zl in range(2)]
Y_GROUPS = [[y * 2 + zl for y in range(NY)] for zl in range(2)]
X_GROUPS = [[t_index(z, x, c) for x in range(NX)] for z in range(NZ) for c in range(NC)]


def over_tensor(value, move):
    return lax.ppermute(value, "tensor", [(t_index(*p), t_index(*move(*p))) for p in all_t()])


def over_y(value, move):
    return lax.ppermute(
        value, "segment", [(y * 2 + zl, (move(y) % NY) * 2 + zl) for y in range(NY) for zl in range(2)]
    )


def core_swap(value):
    return over_tensor(value, lambda z, x, c: (z, x, c ^ 1))


def zl_swap(value):
    return lax.ppermute(value, "segment", [(i, i ^ 1) for i in range(16)])


def transposition(value):
    pairs = []
    for yy in range(NY):
        for zl in range(2):
            for z, x, c in all_t():
                y = z * 2 + (x >> 1)
                there = t_index(yy >> 1, (yy & 1) * 2 + (x & 1), c)
                pairs.append(((yy * 2 + zl) * 32 + t_index(z, x, c), (y * 2 + zl) * 32 + there))
    return lax.ppermute(value, ("segment", "tensor"), pairs)


def stack(*values):
    return jnp.concatenate(values, axis=0)


def together(*values):
    return lax.optimization_barrier(values)


def gather(value, axis, groups):
    return lax.all_gather(value, axis, axis=0, tiled=True, axis_index_groups=groups)


def z_gather(value):
    return gather(value, "tensor", Z_GROUPS)


def x_gather(value):
    return gather(value, "tensor", X_GROUPS)


def whole(shape):
    return pl.BlockSpec(shape, lambda i: (0,) * len(shape))


def scaled_weights(weights, gain):
    return (weights.astype(jnp.float32) * gain).astype(jnp.bfloat16)


def feature_start(z, x, c):
    return pl.multiple_of((z * 8 + x * 2 + c) * PIECE, PIECE)


def hidden_rows(where_ref, own_ref, other_ref, weight_ref, mine_ref, full):
    core = where_ref[0]
    stride = own_ref.shape[0] // NX
    square = jnp.zeros((8, ROWS), jnp.float32)
    for ref, c in ((own_ref, core), (other_ref, core ^ 1)):
        for x in range(NX):
            for z in range(NZ):
                source = x * stride + z * PIECE
                piece = ref[source : source + PIECE, :]
                full[pl.ds(feature_start(z, x, c), PIECE), :] = piece
                wide = piece.astype(jnp.float32)
                square += jnp.sum((wide * wide).reshape(PIECE // 8, 8, ROWS), axis=0)
    mean_square = jnp.sum(square, axis=0, keepdims=True) * (1.0 / WIDTH)
    scale = lax.rsqrt(mean_square + EPSILON)
    hidden = jnp.dot(weight_ref[...], full[...], preferred_element_type=jnp.float32) * scale
    silu = hidden / (1.0 + jnp.exp(-hidden))
    return (mine_ref[...].astype(jnp.float32) + silu).astype(jnp.bfloat16)


def first_tick_kernel(where_ref, own_ref, other_ref, weight_ref, mine_ref, out_ref, full):
    out_ref[...] = hidden_rows(where_ref, own_ref, other_ref, weight_ref, mine_ref, full)


def second_tick_kernel(
    where_ref, own_ref, other_ref, weight_ref, mine_ref, out_ref, next_ref, full
):
    out = hidden_rows(where_ref, own_ref, other_ref, weight_ref, mine_ref, full)
    out_ref[...] = out
    next_ref[:PIECE, :] = out
    for x in range(NX):
        source = x * RIDE + COLUMN
        next_ref[(x + 1) * PIECE : (x + 2) * PIECE, :] = own_ref[source : source + PIECE, :]


def tick(kernel, out_rows, *operands):
    return pl.pallas_call(
        kernel,
        out_shape=[jax.ShapeDtypeStruct((rows, ROWS), jnp.bfloat16) for rows in out_rows],
        in_specs=[SMEM_SPEC] + [VMEM_SPEC] * (len(operands) - 1),
        out_specs=[VMEM_SPEC] * len(out_rows),
        scratch_shapes=[pltpu.VMEM((WIDTH, ROWS), jnp.bfloat16)],
        compiler_params=pltpu.CompilerParams(vmem_limit_bytes=VMEM_LIMIT),
        name="tick",
    )(*operands)


def predict_kernel(
    where_ref, first_own_ref, first_other_ref, own_ref, other_ref, block_ref, teacher_ref, out_ref, full
):
    core, segment = where_ref[0], where_ref[1]
    for ref, c in ((first_own_ref, core), (first_other_ref, core ^ 1)):
        for z in range(NZ):
            for x in range(NX):
                source = z * RIDE + (x + 1) * PIECE
                full[pl.ds(feature_start(z, x, c), PIECE), :ROWS] = ref[source : source + PIECE, :]
    for ref, c in ((own_ref, core), (other_ref, core ^ 1)):
        for x in range(NX):
            for z in range(NZ):
                source = (x * NZ + z) * PIECE
                full[pl.ds(feature_start(z, x, c), PIECE), ROWS:] = ref[source : source + PIECE, :]
    total = jnp.zeros((COLS, TICKS * ROWS), jnp.float32)
    for y in range(NY):
        for j in range(2):
            owner = y * 2 + ((segment & 1) ^ j)
            total += jnp.dot(
                block_ref[(y * 2 + j) * COLS : (y * 2 + j + 1) * COLS, :],
                full[pl.ds(pl.multiple_of(owner * BLOCK, BLOCK), BLOCK), :],
                preferred_element_type=jnp.float32,
            )
    for tau in range(TICKS):
        difference = total[:, tau * ROWS : (tau + 1) * ROWS] - teacher_ref[tau].astype(jnp.float32)
        out_ref[tau * COLS : (tau + 1) * COLS, :] = difference.astype(jnp.bfloat16)


def predict(where, *operands):
    return pl.pallas_call(
        predict_kernel,
        grid=(1,),
        out_shape=jax.ShapeDtypeStruct((TICKS * COLS, ROWS), jnp.bfloat16),
        in_specs=[SMEM_SPEC] + [whole(v.shape) for v in operands],
        out_specs=whole((TICKS * COLS, ROWS)),
        scratch_shapes=[pltpu.VMEM((WIDTH, TICKS * ROWS), jnp.bfloat16)],
        compiler_params=pltpu.CompilerParams(vmem_limit_bytes=VMEM_LIMIT),
        name="predict",
    )(where, *operands)


def gradient_kernel(where_ref, near_ref, far_ref, rows_ref, keep_ref, send_ref, rows):
    segment = where_ref[1]
    for z, x, c in all_t():
        start = ((x & 1) * 2 + c) * PIECE
        for tau in range(TICKS):
            source = (t_index(z, x, c) * TICKS + tau) * PIECE
            columns = slice(tau * ROWS, (tau + 1) * ROWS)
            rows[z * 2 + (x >> 1), start : start + PIECE, columns] = rows_ref[source : source + PIECE, :]
    half, parity = segment & 1, (segment >> 1) & 1
    for part, out_ref in ((half ^ 1, send_ref), (half, keep_ref)):
        total = jnp.zeros((COLS, BLOCK), jnp.float32)
        for ref, p in ((near_ref, parity), (far_ref, parity ^ 1)):
            for i in range(NY // 2):
                both = [ref[(i * TICKS + tau) * COLS : (i * TICKS + tau + 1) * COLS, :] for tau in range(TICKS)]
                total += lax.dot_general(
                    jnp.concatenate(both, axis=1),
                    rows[2 * i + p, pl.ds(pl.multiple_of(part * BLOCK, BLOCK), BLOCK), :],
                    (((1,), (1,)), ((), ())),
                    preferred_element_type=jnp.float32,
                )
        out_ref[...] = (total * (1.0 / (TICKS * ROWS))).astype(out_ref.dtype)


def gradient(where, *operands):
    return pl.pallas_call(
        gradient_kernel,
        out_shape=(
            jax.ShapeDtypeStruct((COLS, BLOCK), jnp.float32),
            jax.ShapeDtypeStruct((COLS, BLOCK), jnp.bfloat16),
        ),
        grid=(1,),
        in_specs=[SMEM_SPEC] + [whole(v.shape) for v in operands],
        out_specs=(whole((COLS, BLOCK)), whole((COLS, BLOCK))),
        scratch_shapes=[pltpu.VMEM((NY, 2 * BLOCK, TICKS * ROWS), jnp.bfloat16)],
        compiler_params=pltpu.CompilerParams(vmem_limit_bytes=VMEM_LIMIT),
        name="gradient",
    )(where, *operands)


def on_device(entering, fresh_rows, norm_gain, segment_weight, projection, teacher_rows):
    t, segment = lax.axis_index("tensor"), lax.axis_index("segment")
    where = jnp.stack([t & 1, segment]).astype(jnp.int32)
    weights = scaled_weights(segment_weight[0], norm_gain)
    teacher = teacher_rows[0].swapaxes(1, 2)
    entering_t, fresh_t = entering[0].T, fresh_rows[0].T

    mine_block = projection.T
    first = z_gather(entering_t)
    other_block, first = together(zl_swap(mine_block), first)
    blocks = gather(stack(mine_block, other_block), "segment", Y_GROUPS)
    own = x_gather(first)
    (out0,) = tick(first_tick_kernel, (PIECE,), where, own, core_swap(own), weights, entering_t)

    shifted = lax.ppermute(out0, "segment", [(i, i + 1) for i in range(15)])
    mine = jnp.where(segment == 0, fresh_t, shifted)
    column = z_gather(mine)
    turned0 = transposition(together(out0, column)[0])
    own = x_gather(stack(column, out0))
    out1, following = tick(second_tick_kernel, (PIECE, RIDE), where, own, core_swap(own), weights, mine)

    first_own = z_gather(following)
    turned, blocks, first_own = together(stack(turned0, transposition(out1)), blocks, first_own)
    rows = lax.all_gather(turned, "tensor", axis=0, tiled=True)
    own = x_gather(first_own.reshape(NZ, RIDE, ROWS)[:, :PIECE].reshape(COLUMN, ROWS))
    difference = predict(where, first_own, core_swap(first_own), own, core_swap(own), blocks, teacher)

    near = gather(difference, "segment", SECOND_Y_GROUPS)
    keep, send = gradient(where, near, over_y(near, lambda y: y ^ 1), rows)
    total = keep + zl_swap(send).astype(jnp.float32)
    return (out1.T[None], total.T)


def solution(mesh):
    return jax.shard_map(
        on_device,
        mesh=mesh,
        in_specs=(
            P("segment", None, "tensor"),
            P(None, None, "tensor"),
            P("segment", None),
            P("segment", "tensor", None),
            P("segment", "tensor"),
            P("segment", None, None, "tensor"),
        ),
        out_specs=(P("segment", None, "tensor"), P("segment", "tensor")),
        check_vma=False,
    )
```

```python
import jax
import jax.numpy as jnp
from jax import lax
from jax.experimental import pallas as pl
from jax.experimental.pallas import tpu as pltpu
from jax.sharding import PartitionSpec as P

EPSILON = 1e-05
TICKS = 2
NZ, NX, NC, NY = 4, 4, 2, 8
ROWS = 128
PIECE = 192
WIDTH = 6144
COLS = 288
BLOCK = 384
COLUMN = 768
RIDE = 960
VMEM_LIMIT = 32 * 1024 * 1024
SMEM_SPEC = pl.BlockSpec(memory_space=pltpu.SMEM)
VMEM_SPEC = pl.BlockSpec(memory_space=pltpu.VMEM)


def t_index(z, x, c):
    return (z % NZ) * 8 + (x % NX) * 2 + c % NC


def all_t():
    return [(z, x, c) for z in range(NZ) for x in range(NX) for c in range(NC)]


Z_GROUPS = [[t_index(z, x, c) for z in range(NZ)] for x in range(NX) for c in range(NC)]
ZC_GROUPS = [[t_index(z, x, c) for z in range(NZ) for c in range(NC)] for x in range(NX)]
SECOND_Y_GROUPS = [[(2 * i + p) * 2 + zl for i in range(NY // 2)] for p in range(2) for zl in range(2)]
Y_GROUPS = [[y * 2 + zl for y in range(NY)] for zl in range(2)]
X_GROUPS = [[t_index(z, x, c) for x in range(NX)] for z in range(NZ) for c in range(NC)]


def over_tensor(value, move):
    return lax.ppermute(value, "tensor", [(t_index(*p), t_index(*move(*p))) for p in all_t()])


def over_y(value, move):
    return lax.ppermute(
        value, "segment", [(y * 2 + zl, (move(y) % NY) * 2 + zl) for y in range(NY) for zl in range(2)]
    )


def core_swap(value):
    return over_tensor(value, lambda z, x, c: (z, x, c ^ 1))


def zl_swap(value):
    return lax.ppermute(value, "segment", [(i, i ^ 1) for i in range(16)])


def transposition(value):
    pairs = []
    for yy in range(NY):
        for zl in range(2):
            for z, x, c in all_t():
                y = z * 2 + (x >> 1)
                there = t_index(yy >> 1, (yy & 1) * 2 + (x & 1), c)
                pairs.append(((yy * 2 + zl) * 32 + t_index(z, x, c), (y * 2 + zl) * 32 + there))
    return lax.ppermute(value, ("segment", "tensor"), pairs)


def stack(*values):
    return jnp.concatenate(values, axis=0)


def together(*values):
    return lax.optimization_barrier(values)


def gather(value, axis, groups):
    return lax.all_gather(value, axis, axis=0, tiled=True, axis_index_groups=groups)


def z_gather(value):
    return gather(value, "tensor", Z_GROUPS)


def x_gather(value):
    return gather(value, "tensor", X_GROUPS)


def whole(shape):
    return pl.BlockSpec(shape, lambda i: (0,) * len(shape))


def scaled_weights(weights, gain):
    return (weights.astype(jnp.float32) * gain).astype(jnp.bfloat16)


def feature_start(z, x, c):
    return pl.multiple_of((z * 8 + x * 2 + c) * PIECE, PIECE)


def hidden_rows(where_ref, own_ref, other_ref, weight_ref, mine_ref, full):
    core = where_ref[0]
    stride = own_ref.shape[0] // NX
    square = jnp.zeros((8, ROWS), jnp.float32)
    for ref, c in ((own_ref, core), (other_ref, core ^ 1)):
        for x in range(NX):
            for z in range(NZ):
                source = x * stride + z * PIECE
                piece = ref[source : source + PIECE, :]
                full[pl.ds(feature_start(z, x, c), PIECE), :] = piece
                wide = piece.astype(jnp.float32)
                square += jnp.sum((wide * wide).reshape(PIECE // 8, 8, ROWS), axis=0)
    mean_square = jnp.sum(square, axis=0, keepdims=True) * (1.0 / WIDTH)
    scale = lax.rsqrt(mean_square + EPSILON)
    hidden = jnp.dot(weight_ref[...], full[...], preferred_element_type=jnp.float32) * scale
    silu = hidden / (1.0 + jnp.exp(-hidden))
    return (mine_ref[...].astype(jnp.float32) + silu).astype(jnp.bfloat16)


def first_tick_kernel(where_ref, own_ref, other_ref, weight_ref, mine_ref, out_ref, full):
    out_ref[...] = hidden_rows(where_ref, own_ref, other_ref, weight_ref, mine_ref, full)


def second_tick_kernel(
    where_ref, own_ref, other_ref, weight_ref, mine_ref, out_ref, next_ref, full
):
    out = hidden_rows(where_ref, own_ref, other_ref, weight_ref, mine_ref, full)
    out_ref[...] = out
    next_ref[:PIECE, :] = out
    for x in range(NX):
        source = x * RIDE + COLUMN
        next_ref[(x + 1) * PIECE : (x + 2) * PIECE, :] = own_ref[source : source + PIECE, :]


def tick(kernel, out_rows, *operands):
    return pl.pallas_call(
        kernel,
        out_shape=[jax.ShapeDtypeStruct((rows, ROWS), jnp.bfloat16) for rows in out_rows],
        in_specs=[SMEM_SPEC] + [VMEM_SPEC] * (len(operands) - 1),
        out_specs=[VMEM_SPEC] * len(out_rows),
        scratch_shapes=[pltpu.VMEM((WIDTH, ROWS), jnp.bfloat16)],
        compiler_params=pltpu.CompilerParams(vmem_limit_bytes=VMEM_LIMIT),
        name="tick",
    )(*operands)


def predict_kernel(
    where_ref, first_own_ref, first_other_ref, own_ref, other_ref, teacher_ref, block_ref, out_ref, full
):
    core, segment = where_ref[0], where_ref[1]
    for ref, c in ((first_own_ref, core), (first_other_ref, core ^ 1)):
        for z in range(NZ):
            for x in range(NX):
                source = z * RIDE + (x + 1) * PIECE
                full[pl.ds(feature_start(z, x, c), PIECE), :ROWS] = ref[source : source + PIECE, :]
    for ref, c in ((own_ref, core), (other_ref, core ^ 1)):
        for x in range(NX):
            for z in range(NZ):
                source = x * RIDE + z * PIECE
                full[pl.ds(feature_start(z, x, c), PIECE), ROWS:] = ref[source : source + PIECE, :]
    total = jnp.zeros((COLS, TICKS * ROWS), jnp.float32)
    for y in range(NY):
        for j in range(2):
            owner = y * 2 + ((segment & 1) ^ j)
            total += jnp.dot(
                block_ref[(y * 2 + j) * COLS : (y * 2 + j + 1) * COLS, :],
                full[pl.ds(pl.multiple_of(owner * BLOCK, BLOCK), BLOCK), :],
                preferred_element_type=jnp.float32,
            )
    for tau in range(TICKS):
        difference = total[:, tau * ROWS : (tau + 1) * ROWS] - teacher_ref[tau].astype(jnp.float32)
        out_ref[tau * COLS : (tau + 1) * COLS, :] = difference.astype(jnp.bfloat16)


def predict(where, *operands):
    return pl.pallas_call(
        predict_kernel,
        grid=(1,),
        out_shape=jax.ShapeDtypeStruct((TICKS * COLS, ROWS), jnp.bfloat16),
        in_specs=[SMEM_SPEC] + [whole(v.shape) for v in operands],
        out_specs=whole((TICKS * COLS, ROWS)),
        scratch_shapes=[pltpu.VMEM((WIDTH, TICKS * ROWS), jnp.bfloat16)],
        compiler_params=pltpu.CompilerParams(vmem_limit_bytes=VMEM_LIMIT),
        name="predict",
    )(where, *operands)


def gradient_kernel(
    where_ref, near_ref, low_ref, high_ref, rows0_ref, rows1_ref, keep_ref, send_ref, rows
):
    segment = where_ref[1]
    for z, x, c in all_t():
        y, start = z * 2 + (x >> 1), ((x & 1) * 2 + c) * PIECE
        source0, source1 = t_index(z, x, c) * PIECE, ((z * NC + c) * NX + x) * PIECE
        rows[y, start : start + PIECE, :ROWS] = rows0_ref[source0 : source0 + PIECE, :]
        rows[y, start : start + PIECE, ROWS:] = rows1_ref[source1 : source1 + PIECE, :]
    half, parity = segment & 1, (segment >> 1) & 1
    held = [(near_ref, i, i, parity) for i in range(NY // 2)]
    held += [(low_ref, i, i, parity ^ 1) for i in range(2)] + [(high_ref, i, i + 2, parity ^ 1) for i in range(2)]
    for part, out_ref in ((half ^ 1, send_ref), (half, keep_ref)):
        total = jnp.zeros((COLS, BLOCK), jnp.float32)
        for ref, k, i, p in held:
            both = [ref[(k * TICKS + tau) * COLS : (k * TICKS + tau + 1) * COLS, :] for tau in range(TICKS)]
            total += lax.dot_general(
                jnp.concatenate(both, axis=1),
                rows[2 * i + p, pl.ds(pl.multiple_of(part * BLOCK, BLOCK), BLOCK), :],
                (((1,), (1,)), ((), ())),
                preferred_element_type=jnp.float32,
            )
        out_ref[...] = (total * (1.0 / (TICKS * ROWS))).astype(out_ref.dtype)


def gradient(where, *operands):
    return pl.pallas_call(
        gradient_kernel,
        out_shape=(
            jax.ShapeDtypeStruct((COLS, BLOCK), jnp.float32),
            jax.ShapeDtypeStruct((COLS, BLOCK), jnp.bfloat16),
        ),
        grid=(1,),
        in_specs=[SMEM_SPEC] + [whole(v.shape) for v in operands],
        out_specs=(whole((COLS, BLOCK)), whole((COLS, BLOCK))),
        scratch_shapes=[pltpu.VMEM((NY, 2 * BLOCK, TICKS * ROWS), jnp.bfloat16)],
        compiler_params=pltpu.CompilerParams(vmem_limit_bytes=VMEM_LIMIT),
        name="gradient",
    )(where, *operands)


def on_device(entering, fresh_rows, norm_gain, segment_weight, projection, teacher_rows):
    t, segment = lax.axis_index("tensor"), lax.axis_index("segment")
    where = jnp.stack([t & 1, segment]).astype(jnp.int32)
    weights = scaled_weights(segment_weight[0], norm_gain)
    teacher = teacher_rows[0].swapaxes(1, 2)
    entering_t, fresh_t = entering[0].T, fresh_rows[0].T

    mine_block = projection.T
    first = z_gather(entering_t)
    other_block, first = together(zl_swap(mine_block), first)
    blocks = gather(stack(mine_block, other_block), "segment", Y_GROUPS)
    own = x_gather(first)
    (out0,) = tick(first_tick_kernel, (PIECE,), where, own, core_swap(own), weights, entering_t)

    shifted = lax.ppermute(out0, "segment", [(i, i + 1) for i in range(15)])
    mine = jnp.where(segment == 0, fresh_t, shifted)
    column = z_gather(mine)
    own = x_gather(stack(column, out0))
    turned0, own = together(transposition(out0), own)
    rows0 = lax.all_gather(turned0, "tensor", axis=0, tiled=True)
    out1, following = tick(second_tick_kernel, (PIECE, RIDE), where, own, core_swap(own), weights, mine)

    first_own = z_gather(following)
    turned1, blocks, first_own = together(transposition(out1), blocks, first_own)
    column = first_own.reshape(NZ, RIDE, ROWS)[:, :PIECE].reshape(COLUMN, ROWS)
    own, first_other = together(x_gather(stack(column, turned1)), core_swap(first_own))
    other = core_swap(own)
    columns1, _ = together(own.reshape(NX, RIDE, ROWS)[:, COLUMN:].reshape(COLUMN, ROWS), other)
    rows1 = gather(columns1, "tensor", ZC_GROUPS)
    difference = predict(where, first_own, first_other, own, other, teacher, blocks)

    near = gather(difference, "segment", SECOND_Y_GROUPS)
    middle = TICKS * TICKS * COLS
    low = over_y(near[:middle], lambda y: y ^ 1)
    high = over_y(near[middle:], lambda y: y - 1 if y % 2 == 0 else y + 1)
    keep, send = gradient(where, near, low, high, rows0, rows1)
    total = keep + zl_swap(send).astype(jnp.float32)
    return (out1.T[None], total.T)


def solution(mesh):
    return jax.shard_map(
        on_device,
        mesh=mesh,
        in_specs=(
            P("segment", None, "tensor"),
            P(None, None, "tensor"),
            P("segment", None),
            P("segment", "tensor", None),
            P("segment", "tensor"),
            P("segment", None, None, "tensor"),
        ),
        out_specs=(P("segment", None, "tensor"), P("segment", "tensor")),
        check_vma=False,
    )
```

```python
import jax
import jax.numpy as jnp
from jax import lax
from jax.experimental import pallas as pl
from jax.experimental.pallas import tpu as pltpu
from jax.sharding import PartitionSpec as P

EPSILON = 1e-05
TICKS = 2
NZ, NX, NC, NY = 4, 4, 2, 8
ROWS = 128
PIECE = 192
WIDTH = 6144
COLS = 288
BLOCK = 384
COLUMN = 768
RIDE = 960
VMEM_LIMIT = 32 * 1024 * 1024
SMEM_SPEC = pl.BlockSpec(memory_space=pltpu.SMEM)
VMEM_SPEC = pl.BlockSpec(memory_space=pltpu.VMEM)


def t_index(z, x, c):
    return (z % NZ) * 8 + (x % NX) * 2 + c % NC


def all_t():
    return [(z, x, c) for z in range(NZ) for x in range(NX) for c in range(NC)]


Z_GROUPS = [[t_index(z, x, c) for z in range(NZ)] for x in range(NX) for c in range(NC)]
ZC_GROUPS = [[t_index(z, x, c) for z in range(NZ) for c in range(NC)] for x in range(NX)]
SECOND_Y_GROUPS = [[(2 * i + p) * 2 + zl for i in range(NY // 2)] for p in range(2) for zl in range(2)]
Y_GROUPS = [[y * 2 + zl for y in range(NY)] for zl in range(2)]
X_GROUPS = [[t_index(z, x, c) for x in range(NX)] for z in range(NZ) for c in range(NC)]


def over_tensor(value, move):
    return lax.ppermute(value, "tensor", [(t_index(*p), t_index(*move(*p))) for p in all_t()])


def over_y(value, move):
    return lax.ppermute(
        value, "segment", [(y * 2 + zl, (move(y) % NY) * 2 + zl) for y in range(NY) for zl in range(2)]
    )


def core_swap(value):
    return over_tensor(value, lambda z, x, c: (z, x, c ^ 1))


def zl_swap(value):
    return lax.ppermute(value, "segment", [(i, i ^ 1) for i in range(16)])


def transposition(value):
    pairs = []
    for yy in range(NY):
        for zl in range(2):
            for z, x, c in all_t():
                y = z * 2 + (x >> 1)
                there = t_index(yy >> 1, (yy & 1) * 2 + (x & 1), c)
                pairs.append(((yy * 2 + zl) * 32 + t_index(z, x, c), (y * 2 + zl) * 32 + there))
    return lax.ppermute(value, ("segment", "tensor"), pairs)


def stack(*values):
    return jnp.concatenate(values, axis=0)


def together(*values):
    return lax.optimization_barrier(values)


def gather(value, axis, groups):
    return lax.all_gather(value, axis, axis=0, tiled=True, axis_index_groups=groups)


def z_gather(value):
    return gather(value, "tensor", Z_GROUPS)


def x_gather(value):
    return gather(value, "tensor", X_GROUPS)


def whole(shape):
    return pl.BlockSpec(shape, lambda i: (0,) * len(shape))


def scaled_weights(weights, gain):
    return (weights.astype(jnp.float32) * gain).astype(jnp.bfloat16)


def feature_start(z, x, c):
    return pl.multiple_of((z * 8 + x * 2 + c) * PIECE, PIECE)


def hidden_rows(where_ref, own_ref, other_ref, weight_ref, mine_ref, full):
    core = where_ref[0]
    stride = own_ref.shape[0] // NX
    square = jnp.zeros((8, ROWS), jnp.float32)
    for ref, c in ((own_ref, core), (other_ref, core ^ 1)):
        for x in range(NX):
            for z in range(NZ):
                source = x * stride + z * PIECE
                piece = ref[source : source + PIECE, :]
                full[pl.ds(feature_start(z, x, c), PIECE), :] = piece
                wide = piece.astype(jnp.float32)
                square += jnp.sum((wide * wide).reshape(PIECE // 8, 8, ROWS), axis=0)
    mean_square = jnp.sum(square, axis=0, keepdims=True) * (1.0 / WIDTH)
    scale = lax.rsqrt(mean_square + EPSILON)
    hidden = jnp.dot(weight_ref[...], full[...], preferred_element_type=jnp.float32) * scale
    silu = hidden / (1.0 + jnp.exp(-hidden))
    return (mine_ref[...].astype(jnp.float32) + silu).astype(jnp.bfloat16)


def first_tick_kernel(where_ref, own_ref, other_ref, weight_ref, mine_ref, out_ref, full):
    out_ref[...] = hidden_rows(where_ref, own_ref, other_ref, weight_ref, mine_ref, full)


def second_tick_kernel(
    where_ref, own_ref, other_ref, weight_ref, mine_ref, before_ref, out_ref, both_ref, full
):
    out = hidden_rows(where_ref, own_ref, other_ref, weight_ref, mine_ref, full)
    out_ref[...] = out
    both_ref[:PIECE, :] = before_ref[...]
    both_ref[PIECE:, :] = out


def tick(kernel, out_rows, *operands):
    return pl.pallas_call(
        kernel,
        out_shape=[jax.ShapeDtypeStruct((rows, ROWS), jnp.bfloat16) for rows in out_rows],
        in_specs=[SMEM_SPEC] + [VMEM_SPEC] * (len(operands) - 1),
        out_specs=[VMEM_SPEC] * len(out_rows),
        scratch_shapes=[pltpu.VMEM((WIDTH, ROWS), jnp.bfloat16)],
        compiler_params=pltpu.CompilerParams(vmem_limit_bytes=VMEM_LIMIT),
        name="tick",
    )(*operands)


def predict_kernel(where_ref, first_ref, own_ref, other_ref, block_ref, teacher_ref, out_ref, full):
    core, segment = where_ref[0], where_ref[1]
    for z, x, c in all_t():
        source, at = ((z * NC + c) * NX + x) * PIECE, t_index(z, x, c) * PIECE
        full[at : at + PIECE, :ROWS] = first_ref[source : source + PIECE, :]
    for ref, c in ((own_ref, core), (other_ref, core ^ 1)):
        for x in range(NX):
            for z in range(NZ):
                source = (x * NZ + z) * PIECE
                full[pl.ds(feature_start(z, x, c), PIECE), ROWS:] = ref[source : source + PIECE, :]
    total = jnp.zeros((COLS, TICKS * ROWS), jnp.float32)
    for y in range(NY):
        for j in range(2):
            owner = y * 2 + ((segment & 1) ^ j)
            total += jnp.dot(
                block_ref[(y * 2 + j) * COLS : (y * 2 + j + 1) * COLS, :],
                full[pl.ds(pl.multiple_of(owner * BLOCK, BLOCK), BLOCK), :],
                preferred_element_type=jnp.float32,
            )
    for tau in range(TICKS):
        difference = total[:, tau * ROWS : (tau + 1) * ROWS] - teacher_ref[tau].astype(jnp.float32)
        out_ref[tau * COLS : (tau + 1) * COLS, :] = difference.astype(jnp.bfloat16)


def predict(where, *operands):
    return pl.pallas_call(
        predict_kernel,
        grid=(1,),
        out_shape=jax.ShapeDtypeStruct((TICKS * COLS, ROWS), jnp.bfloat16),
        in_specs=[SMEM_SPEC] + [whole(v.shape) for v in operands],
        out_specs=whole((TICKS * COLS, ROWS)),
        scratch_shapes=[pltpu.VMEM((WIDTH, TICKS * ROWS), jnp.bfloat16)],
        compiler_params=pltpu.CompilerParams(vmem_limit_bytes=VMEM_LIMIT),
        name="predict",
    )(where, *operands)


def gradient_kernel(where_ref, near_ref, far_ref, rows_ref, keep_ref, send_ref, rows):
    segment = where_ref[1]
    for z, x, c in all_t():
        start = ((x & 1) * 2 + c) * PIECE
        for tau in range(TICKS):
            source = (t_index(z, x, c) * TICKS + tau) * PIECE
            columns = slice(tau * ROWS, (tau + 1) * ROWS)
            rows[z * 2 + (x >> 1), start : start + PIECE, columns] = rows_ref[source : source + PIECE, :]
    half, parity = segment & 1, (segment >> 1) & 1
    for part, out_ref in ((half ^ 1, send_ref), (half, keep_ref)):
        total = jnp.zeros((COLS, BLOCK), jnp.float32)
        for ref, p in ((near_ref, parity), (far_ref, parity ^ 1)):
            for i in range(NY // 2):
                both = [ref[(i * TICKS + tau) * COLS : (i * TICKS + tau + 1) * COLS, :] for tau in range(TICKS)]
                total += lax.dot_general(
                    jnp.concatenate(both, axis=1),
                    rows[2 * i + p, pl.ds(pl.multiple_of(part * BLOCK, BLOCK), BLOCK), :],
                    (((1,), (1,)), ((), ())),
                    preferred_element_type=jnp.float32,
                )
        out_ref[...] = (total * (1.0 / (TICKS * ROWS))).astype(out_ref.dtype)


def gradient(where, *operands):
    return pl.pallas_call(
        gradient_kernel,
        out_shape=(
            jax.ShapeDtypeStruct((COLS, BLOCK), jnp.float32),
            jax.ShapeDtypeStruct((COLS, BLOCK), jnp.bfloat16),
        ),
        grid=(1,),
        in_specs=[SMEM_SPEC] + [whole(v.shape) for v in operands],
        out_specs=(whole((COLS, BLOCK)), whole((COLS, BLOCK))),
        scratch_shapes=[pltpu.VMEM((NY, 2 * BLOCK, TICKS * ROWS), jnp.bfloat16)],
        compiler_params=pltpu.CompilerParams(vmem_limit_bytes=VMEM_LIMIT),
        name="gradient",
    )(where, *operands)


def on_device(entering, fresh_rows, norm_gain, segment_weight, projection, teacher_rows):
    t, segment = lax.axis_index("tensor"), lax.axis_index("segment")
    where = jnp.stack([t & 1, segment]).astype(jnp.int32)
    weights = scaled_weights(segment_weight[0], norm_gain)
    teacher = teacher_rows[0].swapaxes(1, 2)
    entering_t, fresh_t = entering[0].T, fresh_rows[0].T

    mine_block = projection.T
    first = z_gather(entering_t)
    other_block, first = together(zl_swap(mine_block), first)
    blocks = gather(stack(mine_block, other_block), "segment", Y_GROUPS)
    own = x_gather(first)
    (out0,) = tick(first_tick_kernel, (PIECE,), where, own, core_swap(own), weights, entering_t)

    shifted = lax.ppermute(out0, "segment", [(i, i + 1) for i in range(15)])
    mine = jnp.where(segment == 0, fresh_t, shifted)
    own = x_gather(stack(z_gather(mine), out0))
    column = own.reshape(NX, RIDE, ROWS)[:, COLUMN:].reshape(COLUMN, ROWS)
    first_rows = gather(column, "tensor", ZC_GROUPS)
    out1, both = tick(
        second_tick_kernel, (PIECE, 2 * PIECE), where, own, core_swap(own), weights, mine, out0
    )

    second = z_gather(out1)
    turned, blocks, second = together(transposition(both), blocks, second)
    rows = lax.all_gather(turned, "tensor", axis=0, tiled=True)
    own = x_gather(second)
    difference = predict(where, first_rows, own, core_swap(own), blocks, teacher)

    near = gather(difference, "segment", SECOND_Y_GROUPS)
    keep, send = gradient(where, near, over_y(near, lambda y: y ^ 1), rows)
    total = keep + zl_swap(send).astype(jnp.float32)
    return (out1.T[None], total.T)


def solution(mesh):
    return jax.shard_map(
        on_device,
        mesh=mesh,
        in_specs=(
            P("segment", None, "tensor"),
            P(None, None, "tensor"),
            P("segment", None),
            P("segment", "tensor", None),
            P("segment", "tensor"),
            P("segment", None, None, "tensor"),
        ),
        out_specs=(P("segment", None, "tensor"), P("segment", "tensor")),
        check_vma=False,
    )
```

```python
import jax
import jax.numpy as jnp
from jax import lax
from jax.experimental import pallas as pl
from jax.experimental.pallas import tpu as pltpu
from jax.sharding import PartitionSpec as P

EPSILON = 1e-05
TICKS = 2
NZ, NX, NC, NY = 4, 4, 2, 8
ROWS = 128
PIECE = 192
WIDTH = 6144
COLS = 288
BLOCK = 384
VMEM_LIMIT = 32 * 1024 * 1024
SMEM_SPEC = pl.BlockSpec(memory_space=pltpu.SMEM)
VMEM_SPEC = pl.BlockSpec(memory_space=pltpu.VMEM)


def t_index(z, x, c):
    return (z % NZ) * 8 + (x % NX) * 2 + c % NC


def all_t():
    return [(z, x, c) for z in range(NZ) for x in range(NX) for c in range(NC)]


Z_GROUPS = [[t_index(z, x, c) for z in range(NZ)] for x in range(NX) for c in range(NC)]
SECOND_Y_GROUPS = [[(2 * i + p) * 2 + zl for i in range(NY // 2)] for p in range(2) for zl in range(2)]
Y_GROUPS = [[y * 2 + zl for y in range(NY)] for zl in range(2)]
X_GROUPS = [[t_index(z, x, c) for x in range(NX)] for z in range(NZ) for c in range(NC)]


def over_tensor(value, move):
    return lax.ppermute(value, "tensor", [(t_index(*p), t_index(*move(*p))) for p in all_t()])


def over_y(value, move):
    return lax.ppermute(
        value, "segment", [(y * 2 + zl, (move(y) % NY) * 2 + zl) for y in range(NY) for zl in range(2)]
    )


def core_swap(value):
    return over_tensor(value, lambda z, x, c: (z, x, c ^ 1))


def zl_swap(value):
    return lax.ppermute(value, "segment", [(i, i ^ 1) for i in range(16)])


def to_next_segment(value):
    return lax.ppermute(value, "segment", [(s, (s + 1) % 16) for s in range(16)])


def transposition(value):
    pairs = []
    for yy in range(NY):
        for zl in range(2):
            for z, x, c in all_t():
                y = z * 2 + (x >> 1)
                there = t_index(yy >> 1, (yy & 1) * 2 + (x & 1), c)
                pairs.append(((yy * 2 + zl) * 32 + t_index(z, x, c), (y * 2 + zl) * 32 + there))
    return lax.ppermute(value, ("segment", "tensor"), pairs)


def stack(*values):
    return jnp.concatenate(values, axis=0)


def together(*values):
    return lax.optimization_barrier(values)


def gather(value, axis, groups):
    return lax.all_gather(value, axis, axis=0, tiled=True, axis_index_groups=groups)


def z_gather(value):
    return gather(value, "tensor", Z_GROUPS)


def x_gather(value):
    return gather(value, "tensor", X_GROUPS)


def whole(shape):
    return pl.BlockSpec(shape, lambda i: (0,) * len(shape))


def scaled_weights(weights, gain):
    return (weights.astype(jnp.float32) * gain).astype(jnp.bfloat16)


def feature_start(z, x, c):
    return pl.multiple_of((z * 8 + x * 2 + c) * PIECE, PIECE)


def fill(where_ref, own_ref, other_ref, full, columns):
    core = where_ref[0]
    for ref, c in ((own_ref, core), (other_ref, core ^ 1)):
        for x in range(NX):
            for z in range(NZ):
                source = (x * NZ + z) * PIECE
                full[pl.ds(feature_start(z, x, c), PIECE), columns] = ref[source : source + PIECE, :]


def output_rows(weight_ref, mine_ref, full):
    square = jnp.zeros((8, ROWS), jnp.float32)
    for k in range(WIDTH // PIECE):
        wide = full[k * PIECE : (k + 1) * PIECE, :].astype(jnp.float32)
        square += jnp.sum((wide * wide).reshape(PIECE // 8, 8, ROWS), axis=0)
    mean_square = jnp.sum(square, axis=0, keepdims=True) * (1.0 / WIDTH)
    scale = lax.rsqrt(mean_square + EPSILON)
    hidden = jnp.dot(weight_ref[...], full[...], preferred_element_type=jnp.float32) * scale
    silu = hidden / (1.0 + jnp.exp(-hidden))
    return (mine_ref[...].astype(jnp.float32) + silu).astype(jnp.bfloat16)


def first_tick_kernel(where_ref, own_ref, other_ref, weight_ref, mine_ref, out_ref, full):
    fill(where_ref, own_ref, other_ref, full, slice(0, ROWS))
    out_ref[...] = output_rows(weight_ref, mine_ref, full)


def second_tick_kernel(
    where_ref, own_ref, other_ref, fresh_ref, weight_ref, mine_ref, moved_ref, out_ref, both_ref, full
):
    first = where_ref[1] == 0

    @pl.when(first)
    def _():
        full[...] = fresh_ref[...]

    @pl.when(jnp.logical_not(first))
    def _():
        fill(where_ref, own_ref, other_ref, full, slice(0, ROWS))

    out = output_rows(weight_ref, mine_ref, full)
    out_ref[...] = out
    both_ref[:PIECE, :] = moved_ref[...]
    both_ref[PIECE:, :] = out


def tick(kernel, out_rows, *operands):
    return pl.pallas_call(
        kernel,
        out_shape=[jax.ShapeDtypeStruct((rows, ROWS), jnp.bfloat16) for rows in out_rows],
        in_specs=[SMEM_SPEC] + [VMEM_SPEC] * (len(operands) - 1),
        out_specs=[VMEM_SPEC] * len(out_rows),
        scratch_shapes=[pltpu.VMEM((WIDTH, ROWS), jnp.bfloat16)],
        compiler_params=pltpu.CompilerParams(vmem_limit_bytes=VMEM_LIMIT),
        name="tick",
    )(*operands)


def predict_kernel(
    where_ref, own0_ref, other0_ref, own1_ref, other1_ref, block_ref, taught0_ref, taught1_ref, out_ref, full
):
    segment = where_ref[1]
    fill(where_ref, own0_ref, other0_ref, full, slice(0, ROWS))
    fill(where_ref, own1_ref, other1_ref, full, slice(ROWS, 2 * ROWS))
    total = jnp.zeros((COLS, TICKS * ROWS), jnp.float32)
    for y in range(NY):
        for j in range(2):
            owner = y * 2 + ((segment & 1) ^ j)
            total += jnp.dot(
                block_ref[(y * 2 + j) * COLS : (y * 2 + j + 1) * COLS, :],
                full[pl.ds(pl.multiple_of(owner * BLOCK, BLOCK), BLOCK), :],
                preferred_element_type=jnp.float32,
            )
    for tau, taught in enumerate((taught0_ref[0], taught1_ref[1])):
        difference = total[:, tau * ROWS : (tau + 1) * ROWS] - taught.astype(jnp.float32)
        out_ref[tau * COLS : (tau + 1) * COLS, :] = difference.astype(jnp.bfloat16)


def predict(where, *operands):
    return pl.pallas_call(
        predict_kernel,
        grid=(1,),
        out_shape=jax.ShapeDtypeStruct((TICKS * COLS, ROWS), jnp.bfloat16),
        in_specs=[SMEM_SPEC] + [whole(v.shape) for v in operands],
        out_specs=whole((TICKS * COLS, ROWS)),
        scratch_shapes=[pltpu.VMEM((WIDTH, TICKS * ROWS), jnp.bfloat16)],
        compiler_params=pltpu.CompilerParams(vmem_limit_bytes=VMEM_LIMIT),
        name="predict",
    )(where, *operands)


def gradient_kernel(where_ref, near_ref, far_ref, rows_ref, keep_ref, send_ref, rows):
    segment = where_ref[1]
    for z, x, c in all_t():
        start = ((x & 1) * 2 + c) * PIECE
        for tau in range(TICKS):
            source = (t_index(z, x, c) * TICKS + tau) * PIECE
            columns = slice(tau * ROWS, (tau + 1) * ROWS)
            rows[z * 2 + (x >> 1), start : start + PIECE, columns] = rows_ref[source : source + PIECE, :]
    half, parity = segment & 1, (segment >> 1) & 1
    for part, out_ref in ((half ^ 1, send_ref), (half, keep_ref)):
        total = jnp.zeros((COLS, BLOCK), jnp.float32)
        for ref, p in ((near_ref, parity), (far_ref, parity ^ 1)):
            for i in range(NY // 2):
                both = [ref[(i * TICKS + tau) * COLS : (i * TICKS + tau + 1) * COLS, :] for tau in range(TICKS)]
                total += lax.dot_general(
                    jnp.concatenate(both, axis=1),
                    rows[2 * i + p, pl.ds(pl.multiple_of(part * BLOCK, BLOCK), BLOCK), :],
                    (((1,), (1,)), ((), ())),
                    preferred_element_type=jnp.float32,
                )
        out_ref[...] = (total * (1.0 / (TICKS * ROWS))).astype(out_ref.dtype)


def gradient(where, *operands):
    return pl.pallas_call(
        gradient_kernel,
        out_shape=(
            jax.ShapeDtypeStruct((COLS, BLOCK), jnp.float32),
            jax.ShapeDtypeStruct((COLS, BLOCK), jnp.bfloat16),
        ),
        grid=(1,),
        in_specs=[SMEM_SPEC] + [whole(v.shape) for v in operands],
        out_specs=(whole((COLS, BLOCK)), whole((COLS, BLOCK))),
        scratch_shapes=[pltpu.VMEM((NY, 2 * BLOCK, TICKS * ROWS), jnp.bfloat16)],
        compiler_params=pltpu.CompilerParams(vmem_limit_bytes=VMEM_LIMIT),
        name="gradient",
    )(where, *operands)


def on_device(entering, fresh_rows, norm_gain, segment_weight, projection, teacher_rows):
    t, segment = lax.axis_index("tensor"), lax.axis_index("segment")
    where = jnp.stack([t & 1, segment]).astype(jnp.int32)
    weights = scaled_weights(segment_weight[0], norm_gain)
    teacher = teacher_rows[0].swapaxes(1, 2)
    entering_t, fresh_t = entering[0].T, fresh_rows[0].T

    mine_block = projection.T
    fresh_all = lax.all_gather(fresh_t, "tensor", axis=0, tiled=True)
    first = z_gather(entering_t)
    other_block, first = together(zl_swap(mine_block), first)
    blocks = gather(stack(mine_block, other_block), "segment", Y_GROUPS)
    own = x_gather(first)
    taught0 = to_next_segment(together(teacher, own)[0])
    (out0,) = tick(first_tick_kernel, (PIECE,), where, own, core_swap(own), weights, entering_t)

    moved = to_next_segment(out0)
    moved, taught0 = together(moved, taught0)
    mine = jnp.where(segment == 0, fresh_t, moved)
    own0 = x_gather(z_gather(moved))
    other0 = core_swap(own0)
    out1, both = tick(
        second_tick_kernel, (PIECE, 2 * PIECE), where, own0, other0, fresh_all, weights, mine, moved
    )

    second = z_gather(out1)
    turned, second = together(transposition(both), second)
    rows = lax.all_gather(turned, "tensor", axis=0, tiled=True)
    own1 = x_gather(second)
    difference = predict(where, own0, other0, own1, core_swap(own1), blocks, taught0, teacher)

    near = gather(difference, "segment", SECOND_Y_GROUPS)
    keep, send = gradient(where, near, over_y(near, lambda y: y ^ 1), rows)
    total = keep + zl_swap(send).astype(jnp.float32)
    return (out1.T[None], total.T)


def solution(mesh):
    return jax.shard_map(
        on_device,
        mesh=mesh,
        in_specs=(
            P("segment", None, "tensor"),
            P(None, None, "tensor"),
            P("segment", None),
            P("segment", "tensor", None),
            P("segment", "tensor"),
            P("segment", None, None, "tensor"),
        ),
        out_specs=(P("segment", None, "tensor"), P("segment", "tensor")),
        check_vma=False,
    )
```

```python
import jax
import jax.numpy as jnp
from jax import lax
from jax.experimental import pallas as pl
from jax.experimental.pallas import tpu as pltpu
from jax.sharding import PartitionSpec as P

EPSILON = 1e-05
TICKS = 2
NZ, NX, NC, NY = 4, 4, 2, 8
ROWS = 128
PIECE = 192
WIDTH = 6144
COLS = 288
BLOCK = 384
VMEM_LIMIT = 32 * 1024 * 1024
SMEM_SPEC = pl.BlockSpec(memory_space=pltpu.SMEM)
VMEM_SPEC = pl.BlockSpec(memory_space=pltpu.VMEM)


def t_index(z, x, c):
    return (z % NZ) * 8 + (x % NX) * 2 + c % NC


def all_t():
    return [(z, x, c) for z in range(NZ) for x in range(NX) for c in range(NC)]


Z_GROUPS = [[t_index(z, x, c) for z in range(NZ)] for x in range(NX) for c in range(NC)]
XC_GROUPS = [[t_index(z, x, c) for x in range(NX) for c in range(NC)] for z in range(NZ)]
SECOND_Y_GROUPS = [[(2 * i + p) * 2 + zl for i in range(NY // 2)] for p in range(2) for zl in range(2)]
Y_GROUPS = [[y * 2 + zl for y in range(NY)] for zl in range(2)]
X_GROUPS = [[t_index(z, x, c) for x in range(NX)] for z in range(NZ) for c in range(NC)]


def over_tensor(value, move):
    return lax.ppermute(value, "tensor", [(t_index(*p), t_index(*move(*p))) for p in all_t()])


def over_y(value, move):
    return lax.ppermute(
        value, "segment", [(y * 2 + zl, (move(y) % NY) * 2 + zl) for y in range(NY) for zl in range(2)]
    )


def core_swap(value):
    return over_tensor(value, lambda z, x, c: (z, x, c ^ 1))


def zl_swap(value):
    return lax.ppermute(value, "segment", [(i, i ^ 1) for i in range(16)])


def to_next_segment(value):
    return lax.ppermute(value, "segment", [(s, (s + 1) % 16) for s in range(16)])


def transposition(value):
    pairs = []
    for yy in range(NY):
        for zl in range(2):
            for z, x, c in all_t():
                y = z * 2 + (x >> 1)
                there = t_index(yy >> 1, (yy & 1) * 2 + (x & 1), c)
                pairs.append(((yy * 2 + zl) * 32 + t_index(z, x, c), (y * 2 + zl) * 32 + there))
    return lax.ppermute(value, ("segment", "tensor"), pairs)


def stack(*values):
    return jnp.concatenate(values, axis=0)


def together(*values):
    return lax.optimization_barrier(values)


def gather(value, axis, groups):
    return lax.all_gather(value, axis, axis=0, tiled=True, axis_index_groups=groups)


def z_gather(value):
    return gather(value, "tensor", Z_GROUPS)


def x_gather(value):
    return gather(value, "tensor", X_GROUPS)


def whole(shape):
    return pl.BlockSpec(shape, lambda i: (0,) * len(shape))


def scaled_weights(weights, gain):
    return (weights.astype(jnp.float32) * gain).astype(jnp.bfloat16)


def feature_start(z, x, c):
    return pl.multiple_of((z * 8 + x * 2 + c) * PIECE, PIECE)


def fill(where_ref, own_ref, other_ref, full, columns):
    core = where_ref[0]
    for ref, c in ((own_ref, core), (other_ref, core ^ 1)):
        for x in range(NX):
            for z in range(NZ):
                source = (x * NZ + z) * PIECE
                full[pl.ds(feature_start(z, x, c), PIECE), columns] = ref[source : source + PIECE, :]


def output_rows(weight_ref, mine_ref, full):
    square = jnp.zeros((8, ROWS), jnp.float32)
    for k in range(WIDTH // PIECE):
        wide = full[k * PIECE : (k + 1) * PIECE, :].astype(jnp.float32)
        square += jnp.sum((wide * wide).reshape(PIECE // 8, 8, ROWS), axis=0)
    mean_square = jnp.sum(square, axis=0, keepdims=True) * (1.0 / WIDTH)
    scale = lax.rsqrt(mean_square + EPSILON)
    hidden = jnp.dot(weight_ref[...], full[...], preferred_element_type=jnp.float32) * scale
    silu = hidden / (1.0 + jnp.exp(-hidden))
    return (mine_ref[...].astype(jnp.float32) + silu).astype(jnp.bfloat16)


def first_tick_kernel(where_ref, own_ref, other_ref, weight_ref, mine_ref, out_ref, full):
    fill(where_ref, own_ref, other_ref, full, slice(0, ROWS))
    out_ref[...] = output_rows(weight_ref, mine_ref, full)


def second_tick_kernel(
    where_ref, own_ref, other_ref, fresh_ref, weight_ref, mine_ref, moved_ref, out_ref, both_ref, full
):
    first = where_ref[1] == 0

    @pl.when(first)
    def _():
        for z, x, c in all_t():
            source, at = ((x * NC + c) * NZ + z) * PIECE, t_index(z, x, c) * PIECE
            full[at : at + PIECE, :] = fresh_ref[source : source + PIECE, :]

    @pl.when(jnp.logical_not(first))
    def _():
        fill(where_ref, own_ref, other_ref, full, slice(0, ROWS))

    out = output_rows(weight_ref, mine_ref, full)
    out_ref[...] = out
    both_ref[:PIECE, :] = moved_ref[...]
    both_ref[PIECE:, :] = out


def tick(kernel, out_rows, *operands):
    return pl.pallas_call(
        kernel,
        out_shape=[jax.ShapeDtypeStruct((rows, ROWS), jnp.bfloat16) for rows in out_rows],
        in_specs=[SMEM_SPEC] + [VMEM_SPEC] * (len(operands) - 1),
        out_specs=[VMEM_SPEC] * len(out_rows),
        scratch_shapes=[pltpu.VMEM((WIDTH, ROWS), jnp.bfloat16)],
        compiler_params=pltpu.CompilerParams(vmem_limit_bytes=VMEM_LIMIT),
        name="tick",
    )(*operands)


def predict_kernel(
    where_ref, own0_ref, other0_ref, own1_ref, other1_ref, block_ref, taught0_ref, taught1_ref, out_ref, full
):
    segment = where_ref[1]
    fill(where_ref, own0_ref, other0_ref, full, slice(0, ROWS))
    fill(where_ref, own1_ref, other1_ref, full, slice(ROWS, 2 * ROWS))
    total = jnp.zeros((COLS, TICKS * ROWS), jnp.float32)
    for y in range(NY):
        for j in range(2):
            owner = y * 2 + ((segment & 1) ^ j)
            total += jnp.dot(
                block_ref[(y * 2 + j) * COLS : (y * 2 + j + 1) * COLS, :],
                full[pl.ds(pl.multiple_of(owner * BLOCK, BLOCK), BLOCK), :],
                preferred_element_type=jnp.float32,
            )
    for tau, taught in enumerate((taught0_ref[0], taught1_ref[1])):
        difference = total[:, tau * ROWS : (tau + 1) * ROWS] - taught.astype(jnp.float32)
        out_ref[tau * COLS : (tau + 1) * COLS, :] = difference.astype(jnp.bfloat16)


def predict(where, *operands):
    return pl.pallas_call(
        predict_kernel,
        grid=(1,),
        out_shape=jax.ShapeDtypeStruct((TICKS * COLS, ROWS), jnp.bfloat16),
        in_specs=[SMEM_SPEC] + [whole(v.shape) for v in operands],
        out_specs=whole((TICKS * COLS, ROWS)),
        scratch_shapes=[pltpu.VMEM((WIDTH, TICKS * ROWS), jnp.bfloat16)],
        compiler_params=pltpu.CompilerParams(vmem_limit_bytes=VMEM_LIMIT),
        name="predict",
    )(where, *operands)


def gradient_kernel(where_ref, near_ref, far_ref, rows_ref, keep_ref, send_ref, rows):
    segment = where_ref[1]
    for z, x, c in all_t():
        start = ((x & 1) * 2 + c) * PIECE
        for tau in range(TICKS):
            source = (t_index(z, x, c) * TICKS + tau) * PIECE
            columns = slice(tau * ROWS, (tau + 1) * ROWS)
            rows[z * 2 + (x >> 1), start : start + PIECE, columns] = rows_ref[source : source + PIECE, :]
    half, parity = segment & 1, (segment >> 1) & 1
    for part, out_ref in ((half ^ 1, send_ref), (half, keep_ref)):
        total = jnp.zeros((COLS, BLOCK), jnp.float32)
        for ref, p in ((near_ref, parity), (far_ref, parity ^ 1)):
            for i in range(NY // 2):
                both = [ref[(i * TICKS + tau) * COLS : (i * TICKS + tau + 1) * COLS, :] for tau in range(TICKS)]
                total += lax.dot_general(
                    jnp.concatenate(both, axis=1),
                    rows[2 * i + p, pl.ds(pl.multiple_of(part * BLOCK, BLOCK), BLOCK), :],
                    (((1,), (1,)), ((), ())),
                    preferred_element_type=jnp.float32,
                )
        out_ref[...] = (total * (1.0 / (TICKS * ROWS))).astype(out_ref.dtype)


def gradient(where, *operands):
    return pl.pallas_call(
        gradient_kernel,
        out_shape=(
            jax.ShapeDtypeStruct((COLS, BLOCK), jnp.float32),
            jax.ShapeDtypeStruct((COLS, BLOCK), jnp.bfloat16),
        ),
        grid=(1,),
        in_specs=[SMEM_SPEC] + [whole(v.shape) for v in operands],
        out_specs=(whole((COLS, BLOCK)), whole((COLS, BLOCK))),
        scratch_shapes=[pltpu.VMEM((NY, 2 * BLOCK, TICKS * ROWS), jnp.bfloat16)],
        compiler_params=pltpu.CompilerParams(vmem_limit_bytes=VMEM_LIMIT),
        name="gradient",
    )(where, *operands)


def on_device(entering, fresh_rows, norm_gain, segment_weight, projection, teacher_rows):
    t, segment = lax.axis_index("tensor"), lax.axis_index("segment")
    where = jnp.stack([t & 1, segment]).astype(jnp.int32)
    weights = scaled_weights(segment_weight[0], norm_gain)
    teacher = teacher_rows[0].swapaxes(1, 2)
    entering_t, fresh_t = entering[0].T, fresh_rows[0].T

    mine_block = projection.T
    start = z_gather(stack(entering_t, fresh_t)).reshape(NZ, 2, PIECE, ROWS)
    fresh_all = gather(start[:, 1].reshape(NZ * PIECE, ROWS), "tensor", XC_GROUPS)
    first = start[:, 0].reshape(NZ * PIECE, ROWS)
    own = x_gather(first)
    other_block, own = together(zl_swap(mine_block), own)
    blocks = gather(stack(mine_block, other_block), "segment", Y_GROUPS)
    taught0 = to_next_segment(together(teacher, own)[0])
    (out0,) = tick(first_tick_kernel, (PIECE,), where, own, core_swap(own), weights, entering_t)

    moved = to_next_segment(out0)
    moved, taught0 = together(moved, taught0)
    mine = jnp.where(segment == 0, fresh_t, moved)
    own0 = x_gather(z_gather(moved))
    other0 = core_swap(own0)
    out1, both = tick(
        second_tick_kernel, (PIECE, 2 * PIECE), where, own0, other0, fresh_all, weights, mine, moved
    )

    second = z_gather(out1)
    turned, second = together(transposition(both), second)
    rows = lax.all_gather(turned, "tensor", axis=0, tiled=True)
    own1 = x_gather(second)
    difference = predict(where, own0, other0, own1, core_swap(own1), blocks, taught0, teacher)

    near = gather(difference, "segment", SECOND_Y_GROUPS)
    keep, send = gradient(where, near, over_y(near, lambda y: y ^ 1), rows)
    total = keep + zl_swap(send).astype(jnp.float32)
    return (out1.T[None], total.T)


def solution(mesh):
    return jax.shard_map(
        on_device,
        mesh=mesh,
        in_specs=(
            P("segment", None, "tensor"),
            P(None, None, "tensor"),
            P("segment", None),
            P("segment", "tensor", None),
            P("segment", "tensor"),
            P("segment", None, None, "tensor"),
        ),
        out_specs=(P("segment", None, "tensor"), P("segment", "tensor")),
        check_vma=False,
    )
```

```python
import jax
import jax.numpy as jnp
from jax import lax
from jax.experimental import pallas as pl
from jax.experimental.pallas import tpu as pltpu
from jax.sharding import PartitionSpec as P

EPSILON = 1e-05
TICKS = 2
NZ, NX, NC, NY = 4, 4, 2, 8
ROWS = 128
PIECE = 192
WIDTH = 6144
COLS = 288
BLOCK = 384
VMEM_LIMIT = 32 * 1024 * 1024
SMEM_SPEC = pl.BlockSpec(memory_space=pltpu.SMEM)
VMEM_SPEC = pl.BlockSpec(memory_space=pltpu.VMEM)


def t_index(z, x, c):
    return (z % NZ) * 8 + (x % NX) * 2 + c % NC


def all_t():
    return [(z, x, c) for z in range(NZ) for x in range(NX) for c in range(NC)]


Z_GROUPS = [[t_index(z, x, c) for z in range(NZ)] for x in range(NX) for c in range(NC)]
XC_GROUPS = [[t_index(z, x, c) for x in range(NX) for c in range(NC)] for z in range(NZ)]
SECOND_Y_GROUPS = [[(2 * i + p) * 2 + zl for i in range(NY // 2)] for p in range(2) for zl in range(2)]
Y_GROUPS = [[y * 2 + zl for y in range(NY)] for zl in range(2)]
X_GROUPS = [[t_index(z, x, c) for x in range(NX)] for z in range(NZ) for c in range(NC)]


def over_tensor(value, move):
    return lax.ppermute(value, "tensor", [(t_index(*p), t_index(*move(*p))) for p in all_t()])


def over_y(value, move):
    return lax.ppermute(
        value, "segment", [(y * 2 + zl, (move(y) % NY) * 2 + zl) for y in range(NY) for zl in range(2)]
    )


def core_swap(value):
    return over_tensor(value, lambda z, x, c: (z, x, c ^ 1))


def zl_swap(value):
    return lax.ppermute(value, "segment", [(i, i ^ 1) for i in range(16)])


def to_next_segment(value):
    return lax.ppermute(value, "segment", [(s, (s + 1) % 16) for s in range(16)])


def transposition(value):
    pairs = []
    for yy in range(NY):
        for zl in range(2):
            for z, x, c in all_t():
                y = z * 2 + (x >> 1)
                there = t_index(yy >> 1, (yy & 1) * 2 + (x & 1), c)
                pairs.append(((yy * 2 + zl) * 32 + t_index(z, x, c), (y * 2 + zl) * 32 + there))
    return lax.ppermute(value, ("segment", "tensor"), pairs)


def stack(*values):
    return jnp.concatenate(values, axis=0)


def together(*values):
    return lax.optimization_barrier(values)


def gather(value, axis, groups):
    return lax.all_gather(value, axis, axis=0, tiled=True, axis_index_groups=groups)


def z_gather(value):
    return gather(value, "tensor", Z_GROUPS)


def x_gather(value):
    return gather(value, "tensor", X_GROUPS)


def whole(shape):
    return pl.BlockSpec(shape, lambda i: (0,) * len(shape))


def scaled_weights(weights, gain):
    return (weights.astype(jnp.float32) * gain).astype(jnp.bfloat16)


def feature_start(z, x, c):
    return pl.multiple_of((z * 8 + x * 2 + c) * PIECE, PIECE)


def fill(where_ref, own_ref, other_ref, full, columns):
    core = where_ref[0]
    for ref, c in ((own_ref, core), (other_ref, core ^ 1)):
        for x in range(NX):
            for z in range(NZ):
                source = (x * NZ + z) * PIECE
                full[pl.ds(feature_start(z, x, c), PIECE), columns] = ref[source : source + PIECE, :]


def output_rows(weight_ref, mine_ref, full):
    square = jnp.zeros((8, ROWS), jnp.float32)
    for k in range(WIDTH // PIECE):
        wide = full[k * PIECE : (k + 1) * PIECE, :].astype(jnp.float32)
        square += jnp.sum((wide * wide).reshape(PIECE // 8, 8, ROWS), axis=0)
    mean_square = jnp.sum(square, axis=0, keepdims=True) * (1.0 / WIDTH)
    scale = lax.rsqrt(mean_square + EPSILON)
    hidden = jnp.dot(weight_ref[...], full[...], preferred_element_type=jnp.float32) * scale
    silu = hidden / (1.0 + jnp.exp(-hidden))
    return (mine_ref[...].astype(jnp.float32) + silu).astype(jnp.bfloat16)


def first_tick_kernel(where_ref, own_ref, other_ref, weight_ref, mine_ref, out_ref, full):
    fill(where_ref, own_ref, other_ref, full, slice(0, ROWS))
    out_ref[...] = output_rows(weight_ref, mine_ref, full)


def second_tick_kernel(
    where_ref, own_ref, other_ref, fresh_ref, weight_ref, mine_ref, moved_ref, out_ref, both_ref, full
):
    first = where_ref[1] == 0

    @pl.when(first)
    def _():
        for z, x, c in all_t():
            source, at = ((x * NC + c) * NZ + z) * PIECE, t_index(z, x, c) * PIECE
            full[at : at + PIECE, :] = fresh_ref[source : source + PIECE, :]

    @pl.when(jnp.logical_not(first))
    def _():
        fill(where_ref, own_ref, other_ref, full, slice(0, ROWS))

    out = output_rows(weight_ref, mine_ref, full)
    out_ref[...] = out
    both_ref[:PIECE, :] = moved_ref[...]
    both_ref[PIECE:, :] = out


def tick(kernel, out_rows, *operands):
    return pl.pallas_call(
        kernel,
        out_shape=[jax.ShapeDtypeStruct((rows, ROWS), jnp.bfloat16) for rows in out_rows],
        in_specs=[SMEM_SPEC] + [VMEM_SPEC] * (len(operands) - 1),
        out_specs=[VMEM_SPEC] * len(out_rows),
        scratch_shapes=[pltpu.VMEM((WIDTH, ROWS), jnp.bfloat16)],
        compiler_params=pltpu.CompilerParams(vmem_limit_bytes=VMEM_LIMIT),
        name="tick",
    )(*operands)


def predict_kernel(
    where_ref, own0_ref, other0_ref, own1_ref, other1_ref, block_ref, taught0_ref, taught1_ref, out_ref, full
):
    segment = where_ref[1]
    fill(where_ref, own0_ref, other0_ref, full, slice(0, ROWS))
    fill(where_ref, own1_ref, other1_ref, full, slice(ROWS, 2 * ROWS))
    total = jnp.zeros((COLS, TICKS * ROWS), jnp.float32)
    for y in range(NY):
        for j in range(2):
            owner = y * 2 + ((segment & 1) ^ j)
            total += jnp.dot(
                block_ref[(y * 2 + j) * COLS : (y * 2 + j + 1) * COLS, :],
                full[pl.ds(pl.multiple_of(owner * BLOCK, BLOCK), BLOCK), :],
                preferred_element_type=jnp.float32,
            )
    for tau, taught in enumerate((taught0_ref[0], taught1_ref[1])):
        difference = total[:, tau * ROWS : (tau + 1) * ROWS] - taught.astype(jnp.float32)
        out_ref[tau * COLS : (tau + 1) * COLS, :] = difference.astype(jnp.bfloat16)


def predict(where, *operands):
    return pl.pallas_call(
        predict_kernel,
        grid=(1,),
        out_shape=jax.ShapeDtypeStruct((TICKS * COLS, ROWS), jnp.bfloat16),
        in_specs=[SMEM_SPEC] + [whole(v.shape) for v in operands],
        out_specs=whole((TICKS * COLS, ROWS)),
        scratch_shapes=[pltpu.VMEM((WIDTH, TICKS * ROWS), jnp.bfloat16)],
        compiler_params=pltpu.CompilerParams(vmem_limit_bytes=VMEM_LIMIT),
        name="predict",
    )(where, *operands)


def gradient_kernel(where_ref, near_ref, far_ref, rows_ref, keep_ref, send_ref, rows):
    segment = where_ref[1]
    for z, x, c in all_t():
        start = ((x & 1) * 2 + c) * PIECE
        for tau in range(TICKS):
            source = (t_index(z, x, c) * TICKS + tau) * PIECE
            columns = slice(tau * ROWS, (tau + 1) * ROWS)
            rows[z * 2 + (x >> 1), start : start + PIECE, columns] = rows_ref[source : source + PIECE, :]
    half, parity = segment & 1, (segment >> 1) & 1
    for part, out_ref in ((half ^ 1, send_ref), (half, keep_ref)):
        total = jnp.zeros((COLS, BLOCK), jnp.float32)
        for ref, p in ((near_ref, parity), (far_ref, parity ^ 1)):
            for i in range(NY // 2):
                both = [ref[(i * TICKS + tau) * COLS : (i * TICKS + tau + 1) * COLS, :] for tau in range(TICKS)]
                total += lax.dot_general(
                    jnp.concatenate(both, axis=1),
                    rows[2 * i + p, pl.ds(pl.multiple_of(part * BLOCK, BLOCK), BLOCK), :],
                    (((1,), (1,)), ((), ())),
                    preferred_element_type=jnp.float32,
                )
        out_ref[...] = (total * (1.0 / (TICKS * ROWS))).astype(out_ref.dtype)


def gradient(where, *operands):
    return pl.pallas_call(
        gradient_kernel,
        out_shape=(
            jax.ShapeDtypeStruct((COLS, BLOCK), jnp.float32),
            jax.ShapeDtypeStruct((COLS, BLOCK), jnp.bfloat16),
        ),
        grid=(1,),
        in_specs=[SMEM_SPEC] + [whole(v.shape) for v in operands],
        out_specs=(whole((COLS, BLOCK)), whole((COLS, BLOCK))),
        scratch_shapes=[pltpu.VMEM((NY, 2 * BLOCK, TICKS * ROWS), jnp.bfloat16)],
        compiler_params=pltpu.CompilerParams(vmem_limit_bytes=VMEM_LIMIT),
        name="gradient",
    )(where, *operands)


def on_device(entering, fresh_rows, norm_gain, segment_weight, projection, teacher_rows):
    t, segment = lax.axis_index("tensor"), lax.axis_index("segment")
    where = jnp.stack([t & 1, segment]).astype(jnp.int32)
    weights = scaled_weights(segment_weight[0], norm_gain)
    teacher = teacher_rows[0].swapaxes(1, 2)
    entering_t, fresh_t = entering[0].T, fresh_rows[0].T

    mine_block = projection.T
    start = z_gather(stack(entering_t, fresh_t)).reshape(NZ, 2, PIECE, ROWS)
    fresh_all = gather(start[:, 1].reshape(NZ * PIECE, ROWS), "tensor", XC_GROUPS)
    first = start[:, 0].reshape(NZ * PIECE, ROWS)
    own = x_gather(first)
    other_block, own = together(zl_swap(mine_block), own)
    blocks = gather(stack(mine_block, other_block), "segment", Y_GROUPS)
    taught0 = to_next_segment(together(teacher, own)[0])
    (out0,) = tick(first_tick_kernel, (PIECE,), where, own, core_swap(own), weights, entering_t)

    moved = to_next_segment(out0)
    moved, taught0 = together(moved, taught0)
    mine = jnp.where(segment == 0, fresh_t, moved)
    own0 = x_gather(z_gather(moved))
    other0 = core_swap(own0)
    out1, both = tick(
        second_tick_kernel, (PIECE, 2 * PIECE), where, own0, other0, fresh_all, weights, mine, moved
    )

    turned, out1 = together(transposition(both), out1)
    second = z_gather(out1)
    rows = lax.all_gather(turned, "tensor", axis=0, tiled=True)
    own1 = x_gather(second)
    difference = predict(where, own0, other0, own1, core_swap(own1), blocks, taught0, teacher)

    near = gather(difference, "segment", SECOND_Y_GROUPS)
    keep, send = gradient(where, near, over_y(near, lambda y: y ^ 1), rows)
    total = keep + zl_swap(send).astype(jnp.float32)
    return (out1.T[None], total.T)


def solution(mesh):
    return jax.shard_map(
        on_device,
        mesh=mesh,
        in_specs=(
            P("segment", None, "tensor"),
            P(None, None, "tensor"),
            P("segment", None),
            P("segment", "tensor", None),
            P("segment", "tensor"),
            P("segment", None, None, "tensor"),
        ),
        out_specs=(P("segment", None, "tensor"), P("segment", "tensor")),
        check_vma=False,
    )
```
